32 devices in a mesh: snap: 8 (over z, x), row: 4 (over y, core).
Axes of the slice: x: 2, y: 2, z: 4, core: 2. Of those that a mesh axis runs over, the one named last changes fastest.
Arguments:
- snapshots: float32 [512, 131072], P('snap', 'row'), may hold values from -200 to 200, as said below
Outputs:
- modes: float32 [512, 131072], P(None, ('row', 'snap'))
- factor: float32 [512, 512], replicated
The draws below stay inside these ranges and needn't reach their ends.
Inputs may be any that keep to these rules, and one draw needn't show every extreme that they name: `snapshots`: finite snapshot values.
All inputs are finite; a program needn't handle non-finite values.
Results may differ from the reference program's by a relative error of at most 0.00007.
Values sent between devices are 32-bit elements; how exact they have to be, the bound alone decides.
No kernel may reach another device: no remote copies, remote signals or barrier semaphores. Data moves between devices by JAX's collectives and lax.ppermute only.
A program may use at most 128 MiB of HBM per device.

```python
import math
import jax
import jax.numpy as jnp
from jax import lax

K = 512
CELLS = 131072


def draw_snapshots(key, part):
    keys = jax.random.split(key, 3)
    column_scale = jnp.exp(jax.random.uniform(keys[1], (K, 1), jnp.float32) * jnp.log(10.0))
    cell_scale = jnp.exp(jax.random.uniform(keys[2], (1, CELLS), jnp.float32) * jnp.log(10.0))
    ramp = jnp.arange(CELLS, dtype=jnp.float32) / CELLS
    base = jnp.clip(jax.random.normal(keys[0], (K, CELLS), jnp.float32), -6.0, 6.0)
    rising = jnp.exp(jnp.log(3.0) * ramp)
    return base * column_scale * cell_scale * rising[None, :] / 10.0


def setup_inputs(seed: int = 0) -> dict:
    splits = jax.random.split(jax.random.key(seed), 2)
    snapshots = draw_snapshots(jax.random.fold_in(splits[1], 71), 0)
    return dict(snapshots=snapshots)


def reference(snapshots):
    gram = jnp.dot(snapshots.astype(jnp.float32), snapshots.T.astype(jnp.float32), preferred_element_type=jnp.float32, precision=lax.Precision.HIGHEST)
    lower = jnp.linalg.cholesky(gram)
    solved = jax.scipy.linalg.solve_triangular(lower, snapshots, lower=True)
    root_cells = math.sqrt(CELLS)
    return (solved * root_cells, lower / root_cells)
```

```python
import functools
import math

import jax
import jax.numpy as jnp
from jax import lax
from jax.experimental import pallas as pl
from jax.experimental.pallas import tpu as pltpu
from jax.sharding import PartitionSpec as P

BLK = 128
SUB = 8
FULL = lax.Precision.HIGHEST
VMEM = pl.BlockSpec(memory_space=pltpu.VMEM)


def lower_blocks(size):
    return [(i, j) for i in range(size // BLK) for j in range(i + 1)]


def split(x):
    hi = x.astype(jnp.bfloat16)
    return hi, (x - hi.astype(jnp.float32)).astype(jnp.bfloat16)


def gram_kernel(s_ref, out_ref, acc):
    size = s_ref.shape[0]
    hi, lo = split(s_ref[...])
    part = lax.dot_general(
        hi, jnp.concatenate([hi, lo], axis=0), (((1,), (1,)), ((), ())), preferred_element_type=jnp.float32
    )

    @pl.when(pl.program_id(0) == 0)
    def _():
        acc[...] = part

    @pl.when(pl.program_id(0) > 0)
    def _():
        acc[...] += part

    @pl.when(pl.program_id(0) == pl.num_programs(0) - 1)
    def _():
        for n, (i, j) in enumerate(lower_blocks(size)):
            high = acc[i * BLK : (i + 1) * BLK, j * BLK : (j + 1) * BLK]
            mixed = acc[i * BLK : (i + 1) * BLK, size + j * BLK : size + (j + 1) * BLK]
            other = acc[j * BLK : (j + 1) * BLK, size + i * BLK : size + (i + 1) * BLK]
            out_ref[n * BLK : (n + 1) * BLK, :] = high + mixed + other.T


def gram(s, tile):
    size, cells = s.shape
    rows = len(lower_blocks(size)) * BLK
    return pl.pallas_call(
        gram_kernel,
        grid=(cells // tile,),
        out_shape=jax.ShapeDtypeStruct((rows, BLK), jnp.float32),
        in_specs=[pl.BlockSpec((size, tile), lambda i: (0, i))],
        out_specs=pl.BlockSpec((rows, BLK), lambda i: (0, 0)),
        scratch_shapes=[pltpu.VMEM((size, 2 * size), jnp.float32)],
        compiler_params=pltpu.CompilerParams(vmem_limit_bytes=32 * 2**20),
        cost_estimate=pl.CostEstimate(flops=4 * size * size * cells, bytes_accessed=4 * size * cells, transcendentals=0),
        name="gram",
    )(s)


def exchange(x, axis, bit):
    n = lax.axis_size(axis)
    return lax.ppermute(x, axis, [(i, i ^ bit) for i in range(n)])


def bits(axis):
    n = lax.axis_size(axis)
    return [1 << b for b in range(n.bit_length() - 1)]


def sum_all(x):
    for bit in bits("row"):
        upper = (lax.axis_index("row") & bit) > 0
        half = x.shape[0] // 2
        first, second = x[:half], x[half:]
        x = jnp.where(upper, second, first) + exchange(jnp.where(upper, first, second), "row", bit)
    for bit in bits("snap"):
        x = x + exchange(x, "snap", bit)
    for bit in reversed(bits("row")):
        upper = (lax.axis_index("row") & bit) > 0
        got = exchange(x, "row", bit)
        x = jnp.where(upper, jnp.concatenate([got, x]), jnp.concatenate([x, got]))
    return x


def recip(d):
    r = pl.reciprocal(d, approx=True)
    return r * (2.0 - d * r)


def factor_block(load, store_x, store_u):
    groups = BLK // SUB
    lane = lax.broadcasted_iota(jnp.int32, (SUB, BLK), 1)
    sub = lax.broadcasted_iota(jnp.int32, (SUB, BLK), 0)
    rows = [load(i) for i in range(groups)]
    for k in range(groups):
        base = SUB * k
        panel = rows[k]

        def columns(x):
            return [jnp.broadcast_to(x[:, base + j : base + j + 1], (SUB, BLK)) for j in range(SUB)]

        spread = columns(panel)
        cell = {(i, j): jnp.broadcast_to(spread[j][i : i + 1, :], (SUB, BLK)) for i in range(SUB) for j in range(i + 1)}
        inv, ratio = [], {}
        for j in range(SUB):
            inv.append(recip(cell[j, j]))
            for i in range(j + 1, SUB):
                ratio[i, j] = cell[i, j] * inv[j]
            for i in range(j + 1, SUB):
                for c in range(j + 1, i + 1):
                    cell[i, c] = cell[i, c] - ratio[i, j] * cell[c, j]

        def multipliers(cols):
            out = []
            for j in range(SUB):
                for c in range(j + 1, SUB):
                    cols[c] = cols[c] - cols[j] * ratio[c, j]
                out.append(cols[j] * inv[j])
            return out

        own = [jnp.where(sub > j, m, 0.0) for j, m in enumerate(multipliers(list(spread)))]
        in_block = (lane >= base) & (lane < base + SUB)
        aug = jnp.where(in_block, jnp.where(lane - base == sub, 1.0, 0.0), panel)
        up = panel
        pivots = jnp.zeros((SUB, BLK), jnp.float32)
        pivot_rows = []
        for j in range(SUB):
            row = jnp.broadcast_to(aug[j : j + 1, :], (SUB, BLK))
            pivot_rows.append(row)
            if j < SUB - 1:
                aug = aug - own[j] * row
                up = up - own[j] * jnp.broadcast_to(up[j : j + 1, :], (SUB, BLK))
            pivots = jnp.where(sub == j, cell[j, j], pivots)
        for i in range(k + 1, groups):
            m = multipliers(columns(rows[i]))
            acc = [m[j] * pivot_rows[j] for j in range(SUB)]
            while len(acc) > 1:
                acc = [acc[2 * t] + acc[2 * t + 1] for t in range(len(acc) // 2)]
            rows[i] = jnp.where(in_block, 0.0, rows[i]) - acc[0]
        scale = lax.rsqrt(pivots)
        store_x(k, jnp.where(lane <= base + sub, aug * scale, 0.0))
        store_u(k, jnp.where(lane >= base + sub, up * scale, 0.0))


def factor_kernel(root, gram_ref, lower_ref, white_ref, work, xs, us, left):
    size = lower_ref.shape[0]
    for n, (i, j) in enumerate(lower_blocks(size)):
        block = gram_ref[n * BLK : (n + 1) * BLK, :]
        work[i * BLK : (i + 1) * BLK, j * BLK : (j + 1) * BLK] = block
        if i != j:
            work[j * BLK : (j + 1) * BLK, i * BLK : (i + 1) * BLK] = block.T
    col = lax.broadcasted_iota(jnp.int32, (BLK, size), 1)
    eye = jnp.where(
        lax.broadcasted_iota(jnp.int32, (BLK, BLK), 0) == lax.broadcasted_iota(jnp.int32, (BLK, BLK), 1), 1.0, 0.0
    )

    def outer(b, carry):
        at = pl.multiple_of(b * BLK, BLK)
        here = pl.ds(at, BLK)

        def load(i):
            return work[pl.ds(pl.multiple_of(at + SUB * i, SUB), SUB), here]

        def store_x(k, v):
            xs[pl.ds(SUB * k, SUB), :] = v

        def store_u(k, v):
            us[pl.ds(SUB * k, SUB), :] = v

        factor_block(load, store_x, store_u)
        work[here, here] = eye
        y = jnp.dot(xs[...], work[here, :], precision=FULL, preferred_element_type=jnp.float32)
        work[here, :] = y
        white_ref[here, :] = jnp.where(col < at + BLK, y, 0.0) * root
        left[...] = jnp.where(col >= at + BLK, y, 0.0).T
        lower_ref[:, here] = left[...] * (1.0 / root)
        lower_ref[here, here] = us[...].T * (1.0 / root)
        for i in range(1, size // BLK):

            @pl.when(i > b)
            def _(i=i):
                sl = pl.ds(i * BLK, BLK)
                work[sl, here] = jnp.zeros((BLK, BLK), jnp.float32)
                work[sl, :] = work[sl, :] - jnp.dot(left[sl, :], y, precision=FULL, preferred_element_type=jnp.float32)

        return carry

    lax.fori_loop(0, size // BLK, outer, 0)


def factorize(packed, size, root):
    out = jax.ShapeDtypeStruct((size, size), jnp.float32)
    return pl.pallas_call(
        functools.partial(factor_kernel, root),
        out_shape=(out, out),
        in_specs=[VMEM],
        out_specs=(VMEM, VMEM),
        scratch_shapes=[
            pltpu.VMEM((size, size), jnp.float32),
            pltpu.VMEM((BLK, BLK), jnp.float32),
            pltpu.VMEM((BLK, BLK), jnp.float32),
            pltpu.VMEM((size, BLK), jnp.float32),
        ],
        compiler_params=pltpu.CompilerParams(vmem_limit_bytes=24 * 2**20),
        name="factor",
    )(packed)


def modes_kernel(w_ref, s_ref, out_ref, w_hi, w_lo):
    size = w_ref.shape[0]

    @pl.when(pl.program_id(0) == 0)
    def _():
        w_hi[...], w_lo[...] = split(w_ref[...])

    hi, lo = split(s_ref[...])
    half = size // 2
    for rows, depth in ((slice(0, half), half), (slice(half, size), size)):
        a, b = w_hi[rows, :depth], w_lo[rows, :depth]
        out_ref[rows, :] = (
            jnp.dot(a, hi[:depth], preferred_element_type=jnp.float32)
            + jnp.dot(a, lo[:depth], preferred_element_type=jnp.float32)
            + jnp.dot(b, hi[:depth], preferred_element_type=jnp.float32)
        )


def whiten(w, s, tile):
    size, cells = s.shape
    return pl.pallas_call(
        modes_kernel,
        grid=(cells // tile,),
        out_shape=jax.ShapeDtypeStruct((size, cells), jnp.float32),
        in_specs=[pl.BlockSpec((size, size), lambda i: (0, 0)), pl.BlockSpec((size, tile), lambda i: (0, i))],
        out_specs=pl.BlockSpec((size, tile), lambda i: (0, i)),
        scratch_shapes=[pltpu.VMEM((size, size), jnp.bfloat16), pltpu.VMEM((size, size), jnp.bfloat16)],
        compiler_params=pltpu.CompilerParams(vmem_limit_bytes=32 * 2**20),
        name="modes",
    )(w, s)


def local(snapshots):
    gathered = lax.all_to_all(snapshots, "snap", split_axis=1, concat_axis=0, tiled=True)
    size, cells = gathered.shape
    root = math.sqrt(cells * lax.axis_size("snap") * lax.axis_size("row"))
    packed = sum_all(gram(gathered, cells // 4))
    factor, white = factorize(packed, size, root)
    return whiten(white, gathered, cells // 8), factor


def solution(mesh):
    in_specs = (P("snap", "row"),)
    out_specs = (P(None, ("row", "snap")), P())
    return jax.shard_map(local, mesh=mesh, in_specs=in_specs, out_specs=out_specs, check_vma=False)
```

```python
import functools
import math

import jax
import jax.numpy as jnp
from jax import lax
from jax.experimental import pallas as pl
from jax.experimental.pallas import tpu as pltpu
from jax.sharding import PartitionSpec as P

BLK = 128
SUB = 8
FULL = lax.Precision.HIGHEST
VMEM = pl.BlockSpec(memory_space=pltpu.VMEM)


def lower_blocks(size):
    return [(i, j) for i in range(size // BLK) for j in range(i + 1)]


def split(x):
    hi = x.astype(jnp.bfloat16)
    return hi, (x - hi.astype(jnp.float32)).astype(jnp.bfloat16)


def gram_kernel(places, first, *refs):
    places_ref, refs = refs[0], refs[1:]
    parts, refs = refs[:places], refs[places:]
    before, (out_ref, hi_ref, lo_ref, acc) = (None, refs) if first else (refs[0], refs[3:])
    rows, size = parts[0].shape[0], hi_ref.shape[0]
    for d, part in enumerate(parts):
        at = pl.ds(pl.multiple_of(places_ref[d] * rows, rows), rows)
        hi_ref[at, :], lo_ref[at, :] = split(part[...])
    hi = hi_ref[...]
    both = jnp.concatenate([hi, lo_ref[...]], axis=0)
    part = lax.dot_general(hi, both, (((1,), (1,)), ((), ())), preferred_element_type=jnp.float32)

    @pl.when(pl.program_id(0) == 0)
    def _():
        acc[...] = part

    @pl.when(pl.program_id(0) > 0)
    def _():
        acc[...] += part

    @pl.when(pl.program_id(0) == pl.num_programs(0) - 1)
    def _():
        for n, (i, j) in enumerate(lower_blocks(size)):
            high = acc[i * BLK : (i + 1) * BLK, j * BLK : (j + 1) * BLK]
            mixed = acc[i * BLK : (i + 1) * BLK, size + j * BLK : size + (j + 1) * BLK]
            other = acc[j * BLK : (j + 1) * BLK, size + i * BLK : size + (i + 1) * BLK]
            total = high + mixed + other.T
            if not first:
                total = total + before[n * BLK : (n + 1) * BLK, :]
            out_ref[n * BLK : (n + 1) * BLK, :] = total


def gram(places, parts, cells, start, tile, earlier=()):
    rows, here = parts[0].shape
    size = rows * len(parts)
    blocks = len(lower_blocks(size)) * BLK
    packed = jax.ShapeDtypeStruct((blocks, BLK), jnp.float32)
    kept = jax.ShapeDtypeStruct((size, cells), jnp.bfloat16)
    any_place = pl.BlockSpec(memory_space=pl.ANY)
    column = pl.BlockSpec((size, tile), lambda i, p: (0, i + start // tile))
    whole = pl.BlockSpec((blocks, BLK), lambda i, p: (0, 0))
    n = len(parts)
    return pl.pallas_call(
        functools.partial(gram_kernel, n, not earlier),
        out_shape=(packed, kept, kept),
        grid_spec=pltpu.PrefetchScalarGridSpec(
            num_scalar_prefetch=1,
            grid=(here // tile,),
            in_specs=[pl.BlockSpec((rows, tile), lambda i, p: (0, i))] * n + ([whole, any_place, any_place] if earlier else []),
            out_specs=(whole, column, column),
            scratch_shapes=[pltpu.VMEM((size, 2 * size), jnp.float32)],
        ),
        input_output_aliases={n + 2: 1, n + 3: 2} if earlier else {},
        compiler_params=pltpu.CompilerParams(vmem_limit_bytes=32 * 2**20),
        cost_estimate=pl.CostEstimate(flops=4 * size * size * here, bytes_accessed=8 * size * here, transcendentals=0),
        name="gram",
    )(places, *parts, *earlier)


def bits(axis):
    n = lax.axis_size(axis)
    return [1 << b for b in range(n.bit_length() - 1)]


def step(x, orders, at):
    rows, snaps = lax.axis_size("row"), lax.axis_size("snap")
    pairs = []
    for r in range(rows):
        for s in range(snaps):
            axis, bit = orders[r % 2][at]
            to = (r ^ bit, s) if axis == "row" else (r, s ^ bit)
            pairs.append((s * rows + r, to[1] * rows + to[0]))
    return lax.ppermute(x, ("snap", "row"), pairs)


def side(orders, at):
    core = lax.axis_index("row") % 2
    flags = [(lax.axis_index(axis) & bit) > 0 for axis, bit in (o[at] for o in orders)]
    return jnp.where(core == 0, flags[0], flags[1])


def sum_all(x):
    links = [("row", b) for b in bits("row")[1:]] + [("snap", b) for b in bits("snap")]
    orders = [[("row", 1), *links], [("row", 1), *links[1:], links[0]]]
    for at in (0, 1):
        upper = side(orders, at)
        half = x.shape[0] // 2
        first, second = x[:half], x[half:]
        x = jnp.where(upper, second, first) + step(jnp.where(upper, first, second), orders, at)
    for at in range(2, len(links) + 1):
        x = x + step(x, orders, at)
    for at in (1, 0):
        upper = side(orders, at)
        got = step(x, orders, at)
        x = jnp.where(upper, jnp.concatenate([got, x]), jnp.concatenate([x, got]))
    return x


def recip(d):
    r = pl.reciprocal(d, approx=True)
    return r * (2.0 - d * r)


def factor_block(load, store_x, store_u):
    groups = BLK // SUB
    lane = lax.broadcasted_iota(jnp.int32, (SUB, BLK), 1)
    sub = lax.broadcasted_iota(jnp.int32, (SUB, BLK), 0)
    rows = [load(i) for i in range(groups)]
    for k in range(groups):
        base = SUB * k
        panel = rows[k]

        def columns(x):
            return [jnp.broadcast_to(x[:, base + j : base + j + 1], (SUB, BLK)) for j in range(SUB)]

        spread = columns(panel)
        cell = {(i, j): jnp.broadcast_to(spread[j][i : i + 1, :], (SUB, BLK)) for i in range(SUB) for j in range(i + 1)}
        inv, ratio = [], {}
        for j in range(SUB):
            inv.append(recip(cell[j, j]))
            for i in range(j + 1, SUB):
                ratio[i, j] = cell[i, j] * inv[j]
            for i in range(j + 1, SUB):
                for c in range(j + 1, i + 1):
                    cell[i, c] = cell[i, c] - ratio[i, j] * cell[c, j]

        def multipliers(cols):
            out = []
            for j in range(SUB):
                for c in range(j + 1, SUB):
                    cols[c] = cols[c] - cols[j] * ratio[c, j]
                out.append(cols[j] * inv[j])
            return out

        own = [jnp.where(sub > j, m, 0.0) for j, m in enumerate(multipliers(list(spread)))]
        in_block = (lane >= base) & (lane < base + SUB)
        aug = jnp.where(in_block, jnp.where(lane - base == sub, 1.0, 0.0), panel)
        up = panel
        pivots = jnp.zeros((SUB, BLK), jnp.float32)
        pivot_rows = []
        for j in range(SUB):
            row = jnp.broadcast_to(aug[j : j + 1, :], (SUB, BLK))
            pivot_rows.append(row)
            if j < SUB - 1:
                aug = aug - own[j] * row
                up = up - own[j] * jnp.broadcast_to(up[j : j + 1, :], (SUB, BLK))
            pivots = jnp.where(sub == j, cell[j, j], pivots)
        for i in range(k + 1, groups):
            m = multipliers(columns(rows[i]))
            acc = [m[j] * pivot_rows[j] for j in range(SUB)]
            while len(acc) > 1:
                acc = [acc[2 * t] + acc[2 * t + 1] for t in range(len(acc) // 2)]
            rows[i] = jnp.where(in_block, 0.0, rows[i]) - acc[0]
        scale = lax.rsqrt(pivots)
        store_x(k, jnp.where(lane <= base + sub, aug * scale, 0.0))
        store_u(k, jnp.where(lane >= base + sub, up * scale, 0.0))


def factor_kernel(root, gram_ref, lower_ref, white_ref, work, xs, us, left):
    size = lower_ref.shape[0]
    for n, (i, j) in enumerate(lower_blocks(size)):
        block = gram_ref[n * BLK : (n + 1) * BLK, :]
        work[i * BLK : (i + 1) * BLK, j * BLK : (j + 1) * BLK] = block
        if i != j:
            work[j * BLK : (j + 1) * BLK, i * BLK : (i + 1) * BLK] = block.T
    col = lax.broadcasted_iota(jnp.int32, (BLK, size), 1)
    eye = jnp.where(
        lax.broadcasted_iota(jnp.int32, (BLK, BLK), 0) == lax.broadcasted_iota(jnp.int32, (BLK, BLK), 1), 1.0, 0.0
    )

    def outer(b, carry):
        at = pl.multiple_of(b * BLK, BLK)
        here = pl.ds(at, BLK)

        def load(i):
            return work[pl.ds(pl.multiple_of(at + SUB * i, SUB), SUB), here]

        def store_x(k, v):
            xs[pl.ds(SUB * k, SUB), :] = v

        def store_u(k, v):
            us[pl.ds(SUB * k, SUB), :] = v

        factor_block(load, store_x, store_u)
        work[here, here] = eye
        y = jnp.dot(xs[...], work[here, :], precision=FULL, preferred_element_type=jnp.float32)
        work[here, :] = y
        white_ref[here, :] = jnp.where(col < at + BLK, y, 0.0) * root
        left[...] = jnp.where(col >= at + BLK, y, 0.0).T
        lower_ref[:, here] = left[...] * (1.0 / root)
        lower_ref[here, here] = us[...].T * (1.0 / root)
        for i in range(1, size // BLK):

            @pl.when(i > b)
            def _(i=i):
                sl = pl.ds(i * BLK, BLK)
                work[sl, here] = jnp.zeros((BLK, BLK), jnp.float32)
                work[sl, :] = work[sl, :] - jnp.dot(left[sl, :], y, precision=FULL, preferred_element_type=jnp.float32)

        return carry

    lax.fori_loop(0, size // BLK, outer, 0)


def factorize(packed, size, root):
    out = jax.ShapeDtypeStruct((size, size), jnp.float32)
    return pl.pallas_call(
        functools.partial(factor_kernel, root),
        out_shape=(out, out),
        in_specs=[VMEM],
        out_specs=(VMEM, VMEM),
        scratch_shapes=[
            pltpu.VMEM((size, size), jnp.float32),
            pltpu.VMEM((BLK, BLK), jnp.float32),
            pltpu.VMEM((BLK, BLK), jnp.float32),
            pltpu.VMEM((size, BLK), jnp.float32),
        ],
        compiler_params=pltpu.CompilerParams(vmem_limit_bytes=24 * 2**20),
        name="factor",
    )(packed)


def modes_kernel(w_ref, hi_ref, lo_ref, out_ref, w_hi, w_lo):
    size = w_ref.shape[0]

    @pl.when(pl.program_id(0) == 0)
    def _():
        w_hi[...], w_lo[...] = split(w_ref[...])

    half = size // 2
    for rows, depth in ((slice(0, half), half), (slice(half, size), size)):
        a, b = w_hi[rows, :depth], w_lo[rows, :depth]
        hi, lo = hi_ref[:depth, :], lo_ref[:depth, :]
        out_ref[rows, :] = (
            jnp.dot(a, hi, preferred_element_type=jnp.float32)
            + jnp.dot(a, lo, preferred_element_type=jnp.float32)
            + jnp.dot(b, hi, preferred_element_type=jnp.float32)
        )


def whiten(w, hi, lo, tile):
    size, cells = hi.shape
    column = pl.BlockSpec((size, tile), lambda i: (0, i))
    return pl.pallas_call(
        modes_kernel,
        grid=(cells // tile,),
        out_shape=jax.ShapeDtypeStruct((size, cells), jnp.float32),
        in_specs=[pl.BlockSpec((size, size), lambda i: (0, 0)), column, column],
        out_specs=column,
        scratch_shapes=[pltpu.VMEM((size, size), jnp.bfloat16), pltpu.VMEM((size, size), jnp.bfloat16)],
        compiler_params=pltpu.CompilerParams(vmem_limit_bytes=32 * 2**20),
        name="modes",
    )(w, hi, lo)


def regroup(snapshots, start, count):
    n = lax.axis_size("snap")
    me = lax.axis_index("snap")
    cells = snapshots.shape[1] // n
    out = []
    for d in range(n):
        block = lax.dynamic_slice_in_dim(snapshots, (me ^ d) * cells + start, count, axis=1)
        out.append(lax.ppermute(block, "snap", [(i, i ^ d) for i in range(n)]) if d else block)
    return out


def local(snapshots):
    n = lax.axis_size("snap")
    size, cells = snapshots.shape[0] * n, snapshots.shape[1] // n
    root = math.sqrt(cells * n * lax.axis_size("row"))
    places = lax.axis_index("snap") ^ jnp.arange(n, dtype=jnp.int32)
    tile = cells // 8
    early = cells - tile
    first = regroup(snapshots, 0, early)
    last = regroup(snapshots, early, tile)
    kept = gram(places, first, cells, 0, tile)
    packed, hi, lo = gram(places, last, cells, early, tile, kept)
    factor, white = factorize(sum_all(packed), size, root)
    return whiten(white, hi, lo, tile), factor


def solution(mesh):
    in_specs = (P("snap", "row"),)
    out_specs = (P(None, ("row", "snap")), P())
    return jax.shard_map(local, mesh=mesh, in_specs=in_specs, out_specs=out_specs, check_vma=False)
```

```python
import functools
import math

import jax
import jax.numpy as jnp
from jax import lax
from jax.experimental import pallas as pl
from jax.experimental.pallas import tpu as pltpu
from jax.sharding import PartitionSpec as P

BLK = 128
SUB = 8
FULL = lax.Precision.HIGHEST
VMEM = pl.BlockSpec(memory_space=pltpu.VMEM)


def lower_blocks(size):
    return [(i, j) for i in range(size // BLK) for j in range(i + 1)]


def split(x):
    hi = x.astype(jnp.bfloat16)
    return hi, (x - hi.astype(jnp.float32)).astype(jnp.bfloat16)


def gram_kernel(count, places_ref, *refs):
    parts, (out_ref, hi_ref, lo_ref) = refs[:count], refs[count:]
    rows, size = parts[0].shape[0], hi_ref.shape[0]
    for d, part in enumerate(parts):
        at = pl.ds(pl.multiple_of(places_ref[d] * rows, rows), rows)
        hi_ref[at, :], lo_ref[at, :] = split(part[...])
    hi = hi_ref[...]
    both = jnp.concatenate([hi, lo_ref[...]], axis=0)
    prod = lax.dot_general(hi, both, (((1,), (1,)), ((), ())), preferred_element_type=jnp.float32)
    for n, (i, j) in enumerate(lower_blocks(size)):
        high = prod[i * BLK : (i + 1) * BLK, j * BLK : (j + 1) * BLK]
        mixed = prod[i * BLK : (i + 1) * BLK, size + j * BLK : size + (j + 1) * BLK]
        other = prod[j * BLK : (j + 1) * BLK, size + i * BLK : size + (i + 1) * BLK]
        out_ref[n * BLK : (n + 1) * BLK, :] = high + mixed + other.T


def gram(places, parts):
    rows, cells = parts[0].shape
    n = len(parts)
    size = rows * n
    kept = jax.ShapeDtypeStruct((size, cells), jnp.bfloat16)
    return pl.pallas_call(
        functools.partial(gram_kernel, n),
        out_shape=(jax.ShapeDtypeStruct((len(lower_blocks(size)) * BLK, BLK), jnp.float32), kept, kept),
        in_specs=[pl.BlockSpec(memory_space=pltpu.SMEM), *[VMEM] * n],
        out_specs=(VMEM, VMEM, VMEM),
        compiler_params=pltpu.CompilerParams(vmem_limit_bytes=48 * 2**20),
        cost_estimate=pl.CostEstimate(flops=4 * size * size * cells, bytes_accessed=8 * size * cells, transcendentals=0),
        name="gram",
    )(places, *parts)


def bits(axis):
    n = lax.axis_size(axis)
    return [1 << b for b in range(n.bit_length() - 1)]


def step(x, orders, at):
    rows, snaps = lax.axis_size("row"), lax.axis_size("snap")
    pairs = []
    for r in range(rows):
        for s in range(snaps):
            axis, bit = orders[r % 2][at]
            to = (r ^ bit, s) if axis == "row" else (r, s ^ bit)
            pairs.append((s * rows + r, to[1] * rows + to[0]))
    return lax.ppermute(x, ("snap", "row"), pairs)


def side(orders, at):
    core = lax.axis_index("row") % 2
    flags = [(lax.axis_index(axis) & bit) > 0 for axis, bit in (o[at] for o in orders)]
    return jnp.where(core == 0, flags[0], flags[1])


def sum_all(x):
    links = [("row", b) for b in bits("row")[1:]] + [("snap", b) for b in bits("snap")]
    orders = [[("row", 1), *links], [("row", 1), *links[1:], links[0]]]
    for at in (0, 1):
        upper = side(orders, at)
        half = x.shape[0] // 2
        first, second = x[:half], x[half:]
        x = jnp.where(upper, second, first) + step(jnp.where(upper, first, second), orders, at)
    for at in range(2, len(links) + 1):
        x = x + step(x, orders, at)
    for at in (1, 0):
        upper = side(orders, at)
        got = step(x, orders, at)
        x = jnp.where(upper, jnp.concatenate([got, x]), jnp.concatenate([x, got]))
    return x


def spread_columns(x, at):
    return [jnp.broadcast_to(x[:, at + j : at + j + 1], (SUB, BLK)) for j in range(SUB)]


def spread_row(x, j):
    return jnp.broadcast_to(x[j : j + 1, :], (SUB, BLK))


def tree_sum(terms):
    while len(terms) > 1:
        terms = [sum(terms[t : t + 2][1:], terms[t]) for t in range(0, len(terms), 2)]
    return terms[0]


def factor_block(rows):
    groups = len(rows)
    part = groups // 2
    lane = lax.broadcasted_iota(jnp.int32, (SUB, BLK), 1)
    sub = lax.broadcasted_iota(jnp.int32, (SUB, BLK), 0)
    rows = list(rows)
    inverse, upper = [], []

    def gather(wide):
        out = wide[0]
        for j in range(1, SUB):
            out = jnp.where(sub == j, wide[j], out)
        return out

    for k in range(groups):
        base = SUB * k
        end = (k // part + 1) * part
        near = k + 1 < end
        if k % part == 0:
            if k:
                top = jnp.concatenate(inverse[k - part : k], axis=0)
                right = jnp.concatenate(upper[k - part : k], axis=0)
                full = jnp.where(lax.broadcasted_iota(jnp.int32, top.shape, 1) < base, top, right)
                rest = lax.dot_general(
                    right[:, base:], full, (((0,), (0,)), ((), ())), precision=FULL, preferred_element_type=jnp.float32
                )
                for i in range(k, groups):
                    old = jnp.where((lane >= base - SUB * part) & (lane < base), 0.0, rows[i])
                    rows[i] = old - rest[SUB * (i - k) : SUB * (i - k + 1), :]
            spread = spread_columns(rows[k], base)
        if near:
            below = spread_columns(rows[k + 1], base)
            beyond = spread_columns(rows[k + 1], base + SUB)
        cell = {(i, j): spread_row(spread[j], i) for i in range(SUB) for j in range(i + 1)}
        in_block = (lane >= base) & (lane < base + SUB)
        up = [spread_row(rows[k], j) for j in range(SUB)]
        aug = [jnp.where(in_block, jnp.where(lane == base + j, 1.0, 0.0), up[j]) for j in range(SUB)]
        inv, ratio = [], {}
        for j in range(SUB):
            inv.append(pl.reciprocal(cell[j, j], approx=True))
            for i in range(j + 1, SUB):
                ratio[i, j] = cell[i, j] * inv[j]
            for i in range(j + 1, SUB):
                for c in range(j + 1, i + 1):
                    cell[i, c] = cell[i, c] - ratio[i, j] * cell[c, j]

        def eliminate(cols):
            cols = list(cols)
            for j in range(SUB):
                for c in range(j + 1, SUB):
                    cols[c] = cols[c] - cols[j] * ratio[c, j]
            return cols

        def update(i, m):
            rows[i] = jnp.where(in_block, 0.0, rows[i]) - tree_sum([m[j] * aug[j] for j in range(SUB)])

        if near:
            below = eliminate(below)
            m = [below[j] * inv[j] for j in range(SUB)]
            spread = [
                beyond[c] - tree_sum([m[j] * spread_row(below[j], c) for j in range(SUB)]) for c in range(SUB)
            ]
        aug, up = eliminate(aug), eliminate(up)
        if near:
            update(k + 1, m)
        for i in range(k + 2, end):
            cols = eliminate(spread_columns(rows[i], base))
            update(i, [cols[j] * inv[j] for j in range(SUB)])
        scale = lax.rsqrt(gather([cell[j, j] for j in range(SUB)]))
        inverse.append(jnp.where(lane <= base + sub, gather(aug) * scale, 0.0))
        upper.append(jnp.where(lane >= base + sub, gather(up) * scale, 0.0))
    return inverse, upper


def factor_kernel(root, gram_ref, lower_ref, white_ref, work, xs, us):
    size = lower_ref.shape[0]
    blocks = size // BLK
    for n, (i, j) in enumerate(lower_blocks(size)):
        block = gram_ref[n * BLK : (n + 1) * BLK, :]
        work[i * BLK : (i + 1) * BLK, j * BLK : (j + 1) * BLK] = block
        if i != j:
            work[j * BLK : (j + 1) * BLK, i * BLK : (i + 1) * BLK] = block.T
    eye = jnp.where(
        lax.broadcasted_iota(jnp.int32, (BLK, BLK), 0) == lax.broadcasted_iota(jnp.int32, (BLK, BLK), 1), 1.0, 0.0
    )
    zero = jnp.zeros((BLK, BLK), jnp.float32)
    for b in range(blocks):
        here = slice(b * BLK, (b + 1) * BLK)
        inverse, upper = factor_block([work[b * BLK + SUB * i : b * BLK + SUB * (i + 1), here] for i in range(BLK // SUB)])
        for k in range(BLK // SUB):
            xs[SUB * k : SUB * (k + 1), :] = inverse[k]
            us[SUB * k : SUB * (k + 1), :] = upper[k]
        work[here, here] = eye
        y = jnp.dot(xs[...], work[here, :], precision=FULL, preferred_element_type=jnp.float32)
        for i in range(b + 1, blocks):
            down = slice(i * BLK, (i + 1) * BLK)
            left = y[:, down].T
            work[down, here] = zero
            work[down, :] = work[down, :] - jnp.dot(left, y, precision=FULL, preferred_element_type=jnp.float32)
            lower_ref[down, here] = left * (1.0 / root)
            lower_ref[here, down] = zero
            white_ref[here, down] = zero
        lower_ref[here, here] = us[...].T * (1.0 / root)
        white_ref[here, : (b + 1) * BLK] = y[:, : (b + 1) * BLK] * root


def factorize(packed, size, root):
    out = jax.ShapeDtypeStruct((size, size), jnp.float32)
    return pl.pallas_call(
        functools.partial(factor_kernel, root),
        out_shape=(out, out),
        in_specs=[VMEM],
        out_specs=(VMEM, VMEM),
        scratch_shapes=[
            pltpu.VMEM((size, size), jnp.float32),
            pltpu.VMEM((BLK, BLK), jnp.float32),
            pltpu.VMEM((BLK, BLK), jnp.float32),
        ],
        compiler_params=pltpu.CompilerParams(vmem_limit_bytes=48 * 2**20),
        name="factor",
    )(packed)


def modes_kernel(w_ref, hi_ref, lo_ref, out_ref, w_hi, w_lo, tiles, sems):
    size, cells = hi_ref.shape
    slots, _, tile = tiles.shape
    half = size // 2
    w_hi[...], w_lo[...] = split(w_ref[...])
    copies = []
    for t in range(cells // tile):
        slot, here = t % slots, slice(t * tile, (t + 1) * tile)
        if t >= slots:
            copies[t - slots].wait()
        for out, depth in ((slice(0, half), half), (slice(half, size), size)):
            a, b = w_hi[out, :depth], w_lo[out, :depth]
            hi, lo = hi_ref[:depth, here], lo_ref[:depth, here]
            tiles[slot, out, :] = (
                jnp.dot(a, hi, preferred_element_type=jnp.float32)
                + jnp.dot(a, lo, preferred_element_type=jnp.float32)
                + jnp.dot(b, hi, preferred_element_type=jnp.float32)
            )
        copies.append(pltpu.make_async_copy(tiles.at[slot], out_ref.at[:, here], sems.at[slot]))
        copies[t].start()
    for copy in copies[-slots:]:
        copy.wait()


def whiten(w, hi, lo, tile, slots):
    size, cells = hi.shape
    return pl.pallas_call(
        modes_kernel,
        out_shape=jax.ShapeDtypeStruct((size, cells), jnp.float32),
        in_specs=[VMEM, VMEM, VMEM],
        out_specs=pl.BlockSpec(memory_space=pl.ANY),
        scratch_shapes=[
            pltpu.VMEM((size, size), jnp.bfloat16),
            pltpu.VMEM((size, size), jnp.bfloat16),
            pltpu.VMEM((slots, size, tile), jnp.float32),
            pltpu.SemaphoreType.DMA((slots,)),
        ],
        compiler_params=pltpu.CompilerParams(vmem_limit_bytes=48 * 2**20),
        name="modes",
    )(w, hi, lo)


def regroup(snapshots):
    n = lax.axis_size("snap")
    me = lax.axis_index("snap")
    cells = snapshots.shape[1] // n
    order = sorted(range(n), key=lambda d: (d < n // 2, (d ^ (n // 4)) if d >= n // 2 else -d))
    parts = []
    for d in order:
        block = lax.dynamic_slice_in_dim(snapshots, (me ^ d) * cells, cells, axis=1)
        parts.append(lax.ppermute(block, "snap", [(i, i ^ d) for i in range(n)]) if d else block)
    return order, parts


def local(snapshots):
    n = lax.axis_size("snap")
    size, cells = snapshots.shape[0] * n, snapshots.shape[1] // n
    root = math.sqrt(cells * n * lax.axis_size("row"))
    order, parts = regroup(snapshots)
    places = lax.axis_index("snap") ^ jnp.array(order, dtype=jnp.int32)
    packed, hi, lo = gram(places, parts)
    factor, white = factorize(sum_all(packed), size, root)
    return whiten(white, hi, lo, cells // 8, 4), factor


def solution(mesh):
    in_specs = (P("snap", "row"),)
    out_specs = (P(None, ("row", "snap")), P())
    return jax.shard_map(local, mesh=mesh, in_specs=in_specs, out_specs=out_specs, check_vma=False)
```

```python
import functools
import math

import jax
import jax.numpy as jnp
from jax import lax
from jax.experimental import pallas as pl
from jax.experimental.pallas import tpu as pltpu
from jax.sharding import PartitionSpec as P

BLK = 128
SUB = 8
FULL = lax.Precision.HIGHEST
VMEM = pl.BlockSpec(memory_space=pltpu.VMEM)
ANY = pl.BlockSpec(memory_space=pl.ANY)
SMEM = pl.BlockSpec(memory_space=pltpu.SMEM)


def lower_blocks(size):
    return [(i, j) for i in range(size // BLK) for j in range(i + 1)]


def split(x):
    hi = x.astype(jnp.bfloat16)
    return hi, (x - hi.astype(jnp.float32)).astype(jnp.bfloat16)


def nt(a, b):
    return lax.dot_general(a, b, (((1,), (1,)), ((), ())), preferred_element_type=jnp.float32)


def gram_kernel(count, tile, places_ref, *refs):
    parts, (out_ref, hi_ref, lo_ref, hi_out, lo_out, acc, sems) = refs[:count], refs[count:]
    rows, cells = parts[0].shape
    size = hi_ref.shape[0]
    stores = []
    for t in range(cells // tile):
        here = slice(t * tile, (t + 1) * tile)
        for d in range(count + 1):
            at = pl.ds(pl.multiple_of(places_ref[d] * rows, rows), rows)
            if d < count:
                hi_ref[at, here], lo_ref[at, here] = split(parts[d][:, here])
            else:
                hi_ref[at, here] = lo_ref[at, here] = jnp.zeros((rows, tile), jnp.bfloat16)
        for ref, out in ((hi_ref, hi_out), (lo_ref, lo_out)):
            stores.append(pltpu.make_async_copy(ref.at[:, here], out.at[:, here], sems.at[len(stores)]))
            stores[-1].start()
        hi = hi_ref[:, here]
        prod = nt(hi, jnp.concatenate([hi, lo_ref[:, here]], axis=0))
        acc[...] = acc[...] + prod if t else prod
    for n, (i, j) in enumerate(lower_blocks(size)):
        high = acc[i * BLK : (i + 1) * BLK, j * BLK : (j + 1) * BLK]
        mixed = acc[i * BLK : (i + 1) * BLK, size + j * BLK : size + (j + 1) * BLK]
        other = acc[j * BLK : (j + 1) * BLK, size + i * BLK : size + (i + 1) * BLK]
        out_ref[n * BLK : (n + 1) * BLK, :] = high + mixed + other.T
    for store in stores:
        store.wait()


def gram(places, parts, tile):
    rows, cells = parts[0].shape
    n = len(parts)
    size = rows * (n + 1)
    kept = jax.ShapeDtypeStruct((size, cells), jnp.bfloat16)
    return pl.pallas_call(
        functools.partial(gram_kernel, n, tile),
        out_shape=(jax.ShapeDtypeStruct((len(lower_blocks(size)) * BLK, BLK), jnp.float32), *[kept] * 4),
        in_specs=[SMEM, *[VMEM] * n],
        out_specs=(VMEM, VMEM, VMEM, ANY, ANY),
        scratch_shapes=[pltpu.VMEM((size, 2 * size), jnp.float32), pltpu.SemaphoreType.DMA((2 * (cells // tile),))],
        compiler_params=pltpu.CompilerParams(vmem_limit_bytes=32 * 2**20),
        cost_estimate=pl.CostEstimate(flops=4 * size * size * cells, bytes_accessed=8 * size * cells, transcendentals=0),
        name="gram",
    )(places, *parts)


def last_kernel(places_ref, before_ref, part_ref, hi_ref, lo_ref, out_ref, hi_last, lo_last, wide):
    rows = part_ref.shape[0]
    size = hi_ref.shape[0]
    place = places_ref[places_ref.shape[0] - 1]
    at = pl.ds(pl.multiple_of(place * rows, rows), rows)
    hi, lo = hi_last[...], lo_last[...] = split(part_ref[...])
    both = jnp.concatenate([hi, lo], axis=0)
    cross = nt(hi_ref[...], both)
    cross = cross[:, :rows] + cross[:, rows:] + nt(lo_ref[...], hi)
    square = nt(hi, both)
    square = square[:, :rows] * 0.5 + square[:, rows:]
    wide[...] = jnp.zeros_like(wide)
    lane = lax.broadcasted_iota(jnp.int32, (rows, size), 1)
    inside = (lane >= place * rows) & (lane < (place + 1) * rows)
    square = jnp.concatenate([square] * (size // rows), axis=1)
    wide[at, :] = cross.T + jnp.where(inside, square, 0.0)
    for n, (i, j) in enumerate(lower_blocks(size)):
        down = wide[i * BLK : (i + 1) * BLK, j * BLK : (j + 1) * BLK]
        across = wide[j * BLK : (j + 1) * BLK, i * BLK : (i + 1) * BLK]
        out_ref[n * BLK : (n + 1) * BLK, :] = before_ref[n * BLK : (n + 1) * BLK, :] + (down + across.T)


def add_last(places, before, part, hi, lo):
    rows, cells = part.shape
    size = hi.shape[0]
    kept = jax.ShapeDtypeStruct((rows, cells), jnp.bfloat16)
    return pl.pallas_call(
        last_kernel,
        out_shape=(jax.ShapeDtypeStruct(before.shape, jnp.float32), kept, kept),
        in_specs=[SMEM, VMEM, VMEM, VMEM, VMEM],
        out_specs=(VMEM, VMEM, VMEM),
        scratch_shapes=[pltpu.VMEM((size, size), jnp.float32)],
        compiler_params=pltpu.CompilerParams(vmem_limit_bytes=16 * 2**20),
        cost_estimate=pl.CostEstimate(flops=6 * rows * size * cells, bytes_accessed=4 * size * cells, transcendentals=0),
        name="gram_last",
    )(places, before, part, hi, lo)


def bits(axis):
    n = lax.axis_size(axis)
    return [1 << b for b in range(n.bit_length() - 1)]


def step(x, orders, at):
    rows, snaps = lax.axis_size("row"), lax.axis_size("snap")
    pairs = []
    for r in range(rows):
        for s in range(snaps):
            axis, bit = orders[r % 2][at]
            to = (r ^ bit, s) if axis == "row" else (r, s ^ bit)
            pairs.append((s * rows + r, to[1] * rows + to[0]))
    return lax.ppermute(x, ("snap", "row"), pairs)


def side(orders, at):
    core = lax.axis_index("row") % 2
    flags = [(lax.axis_index(axis) & bit) > 0 for axis, bit in (o[at] for o in orders)]
    return jnp.where(core == 0, flags[0], flags[1])


def sum_all(x):
    links = [("row", b) for b in bits("row")[1:]] + [("snap", b) for b in bits("snap")]
    orders = [[("row", 1), *links], [("row", 1), *links[1:], links[0]]]
    for at in (0, 1):
        upper = side(orders, at)
        half = x.shape[0] // 2
        first, second = x[:half], x[half:]
        x = jnp.where(upper, second, first) + step(jnp.where(upper, first, second), orders, at)
    for at in range(2, len(links) + 1):
        x = x + step(x, orders, at)
    for at in (1, 0):
        upper = side(orders, at)
        got = step(x, orders, at)
        x = jnp.where(upper, jnp.concatenate([got, x]), jnp.concatenate([x, got]))
    return x


def spread_columns(x, at):
    return [jnp.broadcast_to(x[:, at + j : at + j + 1], (SUB, BLK)) for j in range(SUB)]


def spread_row(x, j):
    return jnp.broadcast_to(x[j : j + 1, :], (SUB, BLK))


def tree_sum(terms):
    while len(terms) > 1:
        terms = [sum(terms[t : t + 2][1:], terms[t]) for t in range(0, len(terms), 2)]
    return terms[0]


def factor_block(rows):
    groups = len(rows)
    part = groups // 2
    lane = lax.broadcasted_iota(jnp.int32, (SUB, BLK), 1)
    sub = lax.broadcasted_iota(jnp.int32, (SUB, BLK), 0)
    rows = list(rows)
    inverse, upper = [], []

    def gather(wide):
        out = wide[0]
        for j in range(1, SUB):
            out = jnp.where(sub == j, wide[j], out)
        return out

    for k in range(groups):
        base = SUB * k
        end = (k // part + 1) * part
        near = k + 1 < end
        if k % part == 0:
            if k:
                top = jnp.concatenate(inverse[k - part : k], axis=0)
                right = jnp.concatenate(upper[k - part : k], axis=0)
                full = jnp.where(lax.broadcasted_iota(jnp.int32, top.shape, 1) < base, top, right)
                rest = lax.dot_general(
                    right[:, base:], full, (((0,), (0,)), ((), ())), precision=FULL, preferred_element_type=jnp.float32
                )
                for i in range(k, groups):
                    old = jnp.where((lane >= base - SUB * part) & (lane < base), 0.0, rows[i])
                    rows[i] = old - rest[SUB * (i - k) : SUB * (i - k + 1), :]
            spread = spread_columns(rows[k], base)
        if near:
            below = spread_columns(rows[k + 1], base)
            beyond = spread_columns(rows[k + 1], base + SUB)
        cell = {(i, j): spread_row(spread[j], i) for i in range(SUB) for j in range(i + 1)}
        in_block = (lane >= base) & (lane < base + SUB)
        up = [spread_row(rows[k], j) for j in range(SUB)]
        aug = [jnp.where(in_block, jnp.where(lane == base + j, 1.0, 0.0), up[j]) for j in range(SUB)]
        inv, ratio = [], {}
        for j in range(SUB):
            inv.append(pl.reciprocal(cell[j, j], approx=True))
            for i in range(j + 1, SUB):
                ratio[i, j] = cell[i, j] * inv[j]
            for i in range(j + 1, SUB):
                for c in range(j + 1, i + 1):
                    cell[i, c] = cell[i, c] - ratio[i, j] * cell[c, j]

        def eliminate(cols):
            cols = list(cols)
            for j in range(SUB):
                for c in range(j + 1, SUB):
                    cols[c] = cols[c] - cols[j] * ratio[c, j]
            return cols

        def update(i, m):
            rows[i] = jnp.where(in_block, 0.0, rows[i]) - tree_sum([m[j] * aug[j] for j in range(SUB)])

        if near:
            below = eliminate(below)
            m = [below[j] * inv[j] for j in range(SUB)]
            spread = [
                beyond[c] - tree_sum([m[j] * spread_row(below[j], c) for j in range(SUB)]) for c in range(SUB)
            ]
        aug, up = eliminate(aug), eliminate(up)
        if near:
            update(k + 1, m)
        for i in range(k + 2, end):
            cols = eliminate(spread_columns(rows[i], base))
            update(i, [cols[j] * inv[j] for j in range(SUB)])
        scale = lax.rsqrt(gather([cell[j, j] for j in range(SUB)]))
        inverse.append(jnp.where(lane <= base + sub, gather(aug) * scale, 0.0))
        upper.append(jnp.where(lane >= base + sub, gather(up) * scale, 0.0))
    return inverse, upper


def factor_kernel(root, gram_ref, lower_ref, white_ref, work, xs, us):
    size = lower_ref.shape[0]
    blocks = size // BLK
    for n, (i, j) in enumerate(lower_blocks(size)):
        block = gram_ref[n * BLK : (n + 1) * BLK, :]
        work[i * BLK : (i + 1) * BLK, j * BLK : (j + 1) * BLK] = block
        if i != j:
            work[j * BLK : (j + 1) * BLK, i * BLK : (i + 1) * BLK] = block.T
    eye = jnp.where(
        lax.broadcasted_iota(jnp.int32, (BLK, BLK), 0) == lax.broadcasted_iota(jnp.int32, (BLK, BLK), 1), 1.0, 0.0
    )
    zero = jnp.zeros((BLK, BLK), jnp.float32)
    for b in range(blocks):
        here = slice(b * BLK, (b + 1) * BLK)
        inverse, upper = factor_block([work[b * BLK + SUB * i : b * BLK + SUB * (i + 1), here] for i in range(BLK // SUB)])
        for k in range(BLK // SUB):
            xs[SUB * k : SUB * (k + 1), :] = inverse[k]
            us[SUB * k : SUB * (k + 1), :] = upper[k]
        work[here, here] = eye
        y = jnp.dot(xs[...], work[here, :], precision=FULL, preferred_element_type=jnp.float32)
        for i in range(b + 1, blocks):
            down = slice(i * BLK, (i + 1) * BLK)
            left = y[:, down].T
            work[down, here] = zero
            work[down, :] = work[down, :] - jnp.dot(left, y, precision=FULL, preferred_element_type=jnp.float32)
            lower_ref[down, here] = left * (1.0 / root)
            lower_ref[here, down] = zero
            white_ref[here, down] = zero
        lower_ref[here, here] = us[...].T * (1.0 / root)
        white_ref[here, : (b + 1) * BLK] = y[:, : (b + 1) * BLK] * root


def factorize(packed, size, root):
    out = jax.ShapeDtypeStruct((size, size), jnp.float32)
    return pl.pallas_call(
        functools.partial(factor_kernel, root),
        out_shape=(out, out),
        in_specs=[VMEM],
        out_specs=(VMEM, VMEM),
        scratch_shapes=[
            pltpu.VMEM((size, size), jnp.float32),
            pltpu.VMEM((BLK, BLK), jnp.float32),
            pltpu.VMEM((BLK, BLK), jnp.float32),
        ],
        compiler_params=pltpu.CompilerParams(vmem_limit_bytes=12 * 2**20),
        cost_estimate=pl.CostEstimate(flops=100 * size**3, bytes_accessed=8 * size * size, transcendentals=size),
        name="factor",
    )(packed)


def modes_kernel(places_ref, w_ref, hi_ref, lo_ref, hi_last, lo_last, out_ref, w_hi, w_lo, s_hi, s_lo, tiles, sems):
    size, cells = hi_ref.shape
    rows = hi_last.shape[0]
    slots, _, tile = tiles.shape
    half = size // 2
    at = pl.ds(pl.multiple_of(places_ref[places_ref.shape[0] - 1] * rows, rows), rows)
    w_hi[...], w_lo[...] = split(w_ref[...])
    copies = []
    for t in range(cells // tile):
        slot, here = t % slots, slice(t * tile, (t + 1) * tile)
        s_hi[t % 2], s_lo[t % 2] = hi_ref[:, here], lo_ref[:, here]
        s_hi[t % 2, at, :], s_lo[t % 2, at, :] = hi_last[:, here], lo_last[:, here]
        if t >= slots:
            copies[t - slots].wait()
        for out, depth in ((slice(0, half), half), (slice(half, size), size)):
            a, b = w_hi[out, :depth], w_lo[out, :depth]
            hi, lo = s_hi[t % 2, :depth, :], s_lo[t % 2, :depth, :]
            tiles[slot, out, :] = (
                jnp.dot(a, hi, preferred_element_type=jnp.float32)
                + jnp.dot(a, lo, preferred_element_type=jnp.float32)
                + jnp.dot(b, hi, preferred_element_type=jnp.float32)
            )
        copies.append(pltpu.make_async_copy(tiles.at[slot], out_ref.at[:, here], sems.at[slot]))
        copies[t].start()
    for copy in copies[-slots:]:
        copy.wait()


def whiten(places, w, hi, lo, hi_last, lo_last, tile, slots):
    size, cells = hi.shape
    return pl.pallas_call(
        modes_kernel,
        out_shape=jax.ShapeDtypeStruct((size, cells), jnp.float32),
        in_specs=[SMEM, *[VMEM] * 5],
        out_specs=ANY,
        scratch_shapes=[
            pltpu.VMEM((size, size), jnp.bfloat16),
            pltpu.VMEM((size, size), jnp.bfloat16),
            pltpu.VMEM((2, size, tile), jnp.bfloat16),
            pltpu.VMEM((2, size, tile), jnp.bfloat16),
            pltpu.VMEM((slots, size, tile), jnp.float32),
            pltpu.SemaphoreType.DMA((slots,)),
        ],
        compiler_params=pltpu.CompilerParams(vmem_limit_bytes=16 * 2**20),
        name="modes",
    )(places, w, hi, lo, hi_last, lo_last)


def regroup(snapshots):
    n = lax.axis_size("snap")
    me = lax.axis_index("snap")
    cells = snapshots.shape[1] // n
    end = n // 2 + n // 4
    got = {}
    for d in sorted(range(n), key=lambda d: (d < n // 2, (d ^ (n // 4)) if d >= n // 2 else -d)):
        block = lax.dynamic_slice_in_dim(snapshots, (me ^ d) * cells, cells, axis=1)
        got[d] = lax.ppermute(block, "snap", [(i, i ^ d) for i in range(n)]) if d else block
    order = [d for d in range(n) if d != end] + [end]
    return me ^ jnp.array(order, dtype=jnp.int32), [got[d] for d in order]


def local(snapshots):
    n = lax.axis_size("snap")
    size, cells = snapshots.shape[0] * n, snapshots.shape[1] // n
    root = math.sqrt(cells * n * lax.axis_size("row"))
    places, parts = regroup(snapshots)
    packed, hi, lo, hi_kept, lo_kept = gram(places, parts[:-1], cells // 8)
    packed, hi_last, lo_last = add_last(places, packed, parts[-1], hi, lo)
    factor, white = factorize(sum_all(packed), size, root)
    return whiten(places, white, hi_kept, lo_kept, hi_last, lo_last, cells // 8, 4), factor


def solution(mesh):
    in_specs = (P("snap", "row"),)
    out_specs = (P(None, ("row", "snap")), P())
    return jax.shard_map(local, mesh=mesh, in_specs=in_specs, out_specs=out_specs, check_vma=False)
```

```python
import functools
import math

import jax
import jax.numpy as jnp
from jax import lax
from jax.experimental import pallas as pl
from jax.experimental.pallas import tpu as pltpu
from jax.sharding import PartitionSpec as P

BLK = 128
SUB = 8
FULL = lax.Precision.HIGHEST
VMEM = pl.BlockSpec(memory_space=pltpu.VMEM)
ANY = pl.BlockSpec(memory_space=pl.ANY)
SMEM = pl.BlockSpec(memory_space=pltpu.SMEM)


def lower_blocks(size):
    return [(i, j) for i in range(size // BLK) for j in range(i + 1)]


def split(x):
    hi = x.astype(jnp.bfloat16)
    return hi, (x - hi.astype(jnp.float32)).astype(jnp.bfloat16)


def nt(a, b):
    return lax.dot_general(a, b, (((1,), (1,)), ((), ())), preferred_element_type=jnp.float32)


def gram_kernel(count, tile, places_ref, *refs):
    parts, (out_ref, hi_ref, lo_ref, hi_out, lo_out, acc, sems) = refs[:count], refs[count:]
    rows, cells = parts[0].shape
    size = hi_ref.shape[0]
    stores = []
    for t in range(cells // tile):
        here = slice(t * tile, (t + 1) * tile)
        for d in range(count + 1):
            at = pl.ds(pl.multiple_of(places_ref[d] * rows, rows), rows)
            if d < count:
                hi_ref[at, here], lo_ref[at, here] = split(parts[d][:, here])
            else:
                hi_ref[at, here] = lo_ref[at, here] = jnp.zeros((rows, tile), jnp.bfloat16)
        for ref, out in ((hi_ref, hi_out), (lo_ref, lo_out)):
            stores.append(pltpu.make_async_copy(ref.at[:, here], out.at[:, here], sems.at[len(stores)]))
            stores[-1].start()
        hi = hi_ref[:, here]
        prod = nt(hi, jnp.concatenate([hi, lo_ref[:, here]], axis=0))
        acc[...] = acc[...] + prod if t else prod
    for n, (i, j) in enumerate(lower_blocks(size)):
        high = acc[i * BLK : (i + 1) * BLK, j * BLK : (j + 1) * BLK]
        mixed = acc[i * BLK : (i + 1) * BLK, size + j * BLK : size + (j + 1) * BLK]
        other = acc[j * BLK : (j + 1) * BLK, size + i * BLK : size + (i + 1) * BLK]
        out_ref[n * BLK : (n + 1) * BLK, :] = high + mixed + other.T
    for store in stores:
        store.wait()


def gram(places, parts, tile):
    rows, cells = parts[0].shape
    n = len(parts)
    size = rows * (n + 1)
    kept = jax.ShapeDtypeStruct((size, cells), jnp.bfloat16)
    return pl.pallas_call(
        functools.partial(gram_kernel, n, tile),
        out_shape=(jax.ShapeDtypeStruct((len(lower_blocks(size)) * BLK, BLK), jnp.float32), *[kept] * 4),
        in_specs=[SMEM, *[VMEM] * n],
        out_specs=(VMEM, VMEM, VMEM, ANY, ANY),
        scratch_shapes=[pltpu.VMEM((size, 2 * size), jnp.float32), pltpu.SemaphoreType.DMA((2 * (cells // tile),))],
        compiler_params=pltpu.CompilerParams(vmem_limit_bytes=32 * 2**20),
        cost_estimate=pl.CostEstimate(flops=4 * size * size * cells, bytes_accessed=8 * size * cells, transcendentals=0),
        name="gram",
    )(places, *parts)


def last_kernel(places_ref, before_ref, part_ref, hi_ref, lo_ref, out_ref, hi_last, lo_last, wide):
    rows = part_ref.shape[0]
    size = hi_ref.shape[0]
    place = places_ref[places_ref.shape[0] - 1]
    at = pl.ds(pl.multiple_of(place * rows, rows), rows)
    hi, lo = hi_last[...], lo_last[...] = split(part_ref[...])
    both = jnp.concatenate([hi, lo], axis=0)
    cross = nt(hi_ref[...], both)
    cross = cross[:, :rows] + cross[:, rows:] + nt(lo_ref[...], hi)
    square = nt(hi, both)
    square = square[:, :rows] * 0.5 + square[:, rows:]
    wide[...] = jnp.zeros_like(wide)
    lane = lax.broadcasted_iota(jnp.int32, (rows, size), 1)
    inside = (lane >= place * rows) & (lane < (place + 1) * rows)
    square = jnp.concatenate([square] * (size // rows), axis=1)
    wide[at, :] = cross.T + jnp.where(inside, square, 0.0)
    for n, (i, j) in enumerate(lower_blocks(size)):
        down = wide[i * BLK : (i + 1) * BLK, j * BLK : (j + 1) * BLK]
        across = wide[j * BLK : (j + 1) * BLK, i * BLK : (i + 1) * BLK]
        out_ref[n * BLK : (n + 1) * BLK, :] = before_ref[n * BLK : (n + 1) * BLK, :] + (down + across.T)


def add_last(places, before, part, hi, lo):
    rows, cells = part.shape
    size = hi.shape[0]
    kept = jax.ShapeDtypeStruct((rows, cells), jnp.bfloat16)
    return pl.pallas_call(
        last_kernel,
        out_shape=(jax.ShapeDtypeStruct(before.shape, jnp.float32), kept, kept),
        in_specs=[SMEM, VMEM, VMEM, VMEM, VMEM],
        out_specs=(VMEM, VMEM, VMEM),
        scratch_shapes=[pltpu.VMEM((size, size), jnp.float32)],
        compiler_params=pltpu.CompilerParams(vmem_limit_bytes=16 * 2**20),
        cost_estimate=pl.CostEstimate(flops=6 * rows * size * cells, bytes_accessed=4 * size * cells, transcendentals=0),
        name="gram_last",
    )(places, before, part, hi, lo)


def bits(axis):
    n = lax.axis_size(axis)
    return [1 << b for b in range(n.bit_length() - 1)]


def step(x, orders, at):
    rows, snaps = lax.axis_size("row"), lax.axis_size("snap")
    pairs = []
    for r in range(rows):
        for s in range(snaps):
            axis, bit = orders[r % 2][at]
            to = (r ^ bit, s) if axis == "row" else (r, s ^ bit)
            pairs.append((s * rows + r, to[1] * rows + to[0]))
    return lax.ppermute(x, ("snap", "row"), pairs)


def side(orders, at):
    core = lax.axis_index("row") % 2
    flags = [(lax.axis_index(axis) & bit) > 0 for axis, bit in (o[at] for o in orders)]
    return jnp.where(core == 0, flags[0], flags[1])


def sum_all(x):
    links = [("row", b) for b in bits("row")[1:]] + [("snap", b) for b in bits("snap")]
    orders = [[("row", 1), *links], [("row", 1), *links[1:], links[0]]]
    for at in (0, 1):
        upper = side(orders, at)
        half = x.shape[0] // 2
        first, second = x[:half], x[half:]
        x = jnp.where(upper, second, first) + step(jnp.where(upper, first, second), orders, at)
    for at in range(2, len(links) + 1):
        x = x + step(x, orders, at)
    for at in (1, 0):
        upper = side(orders, at)
        got = step(x, orders, at)
        x = jnp.where(upper, jnp.concatenate([got, x]), jnp.concatenate([x, got]))
    return x


def spread_columns(x, at):
    return [jnp.broadcast_to(x[:, at + j : at + j + 1], (SUB, BLK)) for j in range(SUB)]


def spread_row(x, j):
    return jnp.broadcast_to(x[j : j + 1, :], (SUB, BLK))


def tree_sum(terms):
    while len(terms) > 1:
        terms = [sum(terms[t : t + 2][1:], terms[t]) for t in range(0, len(terms), 2)]
    return terms[0]


def factor_block(rows):
    groups = len(rows)
    part = groups // 2
    lane = lax.broadcasted_iota(jnp.int32, (SUB, BLK), 1)
    sub = lax.broadcasted_iota(jnp.int32, (SUB, BLK), 0)
    rows = list(rows)
    inverse, upper = [], []

    def gather(wide):
        out = wide[0]
        for j in range(1, SUB):
            out = jnp.where(sub == j, wide[j], out)
        return out

    for k in range(groups):
        base = SUB * k
        end = (k // part + 1) * part
        near = k + 1 < end
        if k % part == 0:
            if k:
                top = jnp.concatenate(inverse[k - part : k], axis=0)
                right = jnp.concatenate(upper[k - part : k], axis=0)
                full = jnp.where(lax.broadcasted_iota(jnp.int32, top.shape, 1) < base, top, right)
                rest = lax.dot_general(
                    right[:, base:], full, (((0,), (0,)), ((), ())), precision=FULL, preferred_element_type=jnp.float32
                )
                for i in range(k, groups):
                    old = jnp.where((lane >= base - SUB * part) & (lane < base), 0.0, rows[i])
                    rows[i] = old - rest[SUB * (i - k) : SUB * (i - k + 1), :]
            spread = spread_columns(rows[k], base)
        if near:
            below = spread_columns(rows[k + 1], base)
            beyond = spread_columns(rows[k + 1], base + SUB)
        cell = {(i, j): spread_row(spread[j], i) for i in range(SUB) for j in range(i + 1)}
        in_block = (lane >= base) & (lane < base + SUB)
        up = [spread_row(rows[k], j) for j in range(SUB)]
        aug = [jnp.where(in_block, jnp.where(lane == base + j, 1.0, 0.0), up[j]) for j in range(SUB)]
        inv, ratio = [], {}
        for j in range(SUB):
            inv.append(pl.reciprocal(cell[j, j], approx=True))
            for i in range(j + 1, SUB):
                ratio[i, j] = cell[i, j] * inv[j]
            for i in range(j + 1, SUB):
                for c in range(j + 1, i + 1):
                    cell[i, c] = cell[i, c] - ratio[i, j] * cell[c, j]

        def eliminate(cols):
            cols = list(cols)
            for j in range(SUB):
                for c in range(j + 1, SUB):
                    cols[c] = cols[c] - cols[j] * ratio[c, j]
            return cols

        def update(i, m):
            rows[i] = jnp.where(in_block, 0.0, rows[i]) - tree_sum([m[j] * aug[j] for j in range(SUB)])

        if near:
            below = eliminate(below)
            m = [below[j] * inv[j] for j in range(SUB)]
            spread = [
                beyond[c] - tree_sum([m[j] * spread_row(below[j], c) for j in range(SUB)]) for c in range(SUB)
            ]
        aug, up = eliminate(aug), eliminate(up)
        if near:
            update(k + 1, m)
        for i in range(k + 2, end):
            cols = eliminate(spread_columns(rows[i], base))
            update(i, [cols[j] * inv[j] for j in range(SUB)])
        scale = lax.rsqrt(gather([cell[j, j] for j in range(SUB)]))
        inverse.append(jnp.where(lane <= base + sub, gather(aug) * scale, 0.0))
        upper.append(jnp.where(lane >= base + sub, gather(up) * scale, 0.0))
    return inverse, upper


def factor_kernel(root, gram_ref, lower_ref, white_ref, work, xs, us):
    size = lower_ref.shape[0]
    blocks = size // BLK
    for n, (i, j) in enumerate(lower_blocks(size)):
        block = gram_ref[n * BLK : (n + 1) * BLK, :]
        work[i * BLK : (i + 1) * BLK, j * BLK : (j + 1) * BLK] = block
        if i != j:
            work[j * BLK : (j + 1) * BLK, i * BLK : (i + 1) * BLK] = block.T
    eye = jnp.where(
        lax.broadcasted_iota(jnp.int32, (BLK, BLK), 0) == lax.broadcasted_iota(jnp.int32, (BLK, BLK), 1), 1.0, 0.0
    )
    zero = jnp.zeros((BLK, BLK), jnp.float32)
    for b in range(blocks):
        here = slice(b * BLK, (b + 1) * BLK)
        inverse, upper = factor_block([work[b * BLK + SUB * i : b * BLK + SUB * (i + 1), here] for i in range(BLK // SUB)])
        for k in range(BLK // SUB):
            xs[SUB * k : SUB * (k + 1), :] = inverse[k]
            us[SUB * k : SUB * (k + 1), :] = upper[k]
        work[here, here] = eye
        y = jnp.dot(xs[...], work[here, :], precision=FULL, preferred_element_type=jnp.float32)
        for i in range(b + 1, blocks):
            down = slice(i * BLK, (i + 1) * BLK)
            left = y[:, down].T
            work[down, here] = zero
            work[down, :] = work[down, :] - jnp.dot(left, y, precision=FULL, preferred_element_type=jnp.float32)
            lower_ref[down, here] = left * (1.0 / root)
            lower_ref[here, down] = zero
            white_ref[here, down] = zero
        lower_ref[here, here] = us[...].T * (1.0 / root)
        white_ref[here, : (b + 1) * BLK] = y[:, : (b + 1) * BLK] * root


def factorize(packed, size, root):
    out = jax.ShapeDtypeStruct((size, size), jnp.float32)
    return pl.pallas_call(
        functools.partial(factor_kernel, root),
        out_shape=(out, out),
        in_specs=[VMEM],
        out_specs=(VMEM, VMEM),
        scratch_shapes=[
            pltpu.VMEM((size, size), jnp.float32),
            pltpu.VMEM((BLK, BLK), jnp.float32),
            pltpu.VMEM((BLK, BLK), jnp.float32),
        ],
        compiler_params=pltpu.CompilerParams(vmem_limit_bytes=12 * 2**20),
        cost_estimate=pl.CostEstimate(flops=100 * size**3, bytes_accessed=8 * size * size, transcendentals=size),
        name="factor",
    )(packed)


def modes_kernel(places_ref, w_ref, hi_ref, lo_ref, hi_last, lo_last, out_ref, w_hi, w_lo, s_hi, s_lo, tiles, sems):
    size, cells = hi_ref.shape
    rows = hi_last.shape[0]
    slots, _, tile = tiles.shape
    half = size // 2
    at = pl.ds(pl.multiple_of(places_ref[places_ref.shape[0] - 1] * rows, rows), rows)
    w_hi[...], w_lo[...] = split(w_ref[...])
    copies = []
    for t in range(cells // tile):
        slot, here = t % slots, slice(t * tile, (t + 1) * tile)
        s_hi[t % 2], s_lo[t % 2] = hi_ref[:, here], lo_ref[:, here]
        s_hi[t % 2, at, :], s_lo[t % 2, at, :] = hi_last[:, here], lo_last[:, here]
        if t >= slots:
            copies[t - slots].wait()
        for out, depth in ((slice(0, half), half), (slice(half, size), size)):
            a, b = w_hi[out, :depth], w_lo[out, :depth]
            hi, lo = s_hi[t % 2, :depth, :], s_lo[t % 2, :depth, :]
            tiles[slot, out, :] = (
                jnp.dot(a, hi, preferred_element_type=jnp.float32)
                + jnp.dot(a, lo, preferred_element_type=jnp.float32)
                + jnp.dot(b, hi, preferred_element_type=jnp.float32)
            )
        copies.append(pltpu.make_async_copy(tiles.at[slot], out_ref.at[:, here], sems.at[slot]))
        copies[t].start()
    for copy in copies[-slots:]:
        copy.wait()


def whiten(places, w, hi, lo, hi_last, lo_last, tile, slots):
    size, cells = hi.shape
    return pl.pallas_call(
        modes_kernel,
        out_shape=jax.ShapeDtypeStruct((size, cells), jnp.float32),
        in_specs=[SMEM, *[VMEM] * 5],
        out_specs=ANY,
        scratch_shapes=[
            pltpu.VMEM((size, size), jnp.bfloat16),
            pltpu.VMEM((size, size), jnp.bfloat16),
            pltpu.VMEM((2, size, tile), jnp.bfloat16),
            pltpu.VMEM((2, size, tile), jnp.bfloat16),
            pltpu.VMEM((slots, size, tile), jnp.float32),
            pltpu.SemaphoreType.DMA((slots,)),
        ],
        compiler_params=pltpu.CompilerParams(vmem_limit_bytes=16 * 2**20),
        name="modes",
    )(places, w, hi, lo, hi_last, lo_last)


def cut_kernel(place_ref, x_ref, out_ref, held, come, go):
    rows, cells = held.shape
    at = pl.ds(pl.multiple_of(place_ref[0] * cells, cells), cells)
    pieces = [slice(SUB * n, SUB * (n + 1)) for n in range(rows // SUB)]
    loads = [pltpu.make_async_copy(x_ref.at[p, at], held.at[p, :], come.at[n]) for n, p in enumerate(pieces)]
    stores = [pltpu.make_async_copy(held.at[p, :], out_ref.at[p, :], go.at[n]) for n, p in enumerate(pieces)]
    for load in loads:
        load.start()
    for load, store in zip(loads, stores, strict=True):
        load.wait()
        store.start()
    for store in stores:
        store.wait()


def cut(place, x, cells):
    rows = x.shape[0]
    return pl.pallas_call(
        cut_kernel,
        out_shape=jax.ShapeDtypeStruct((rows, cells), x.dtype),
        in_specs=[SMEM, ANY],
        out_specs=ANY,
        scratch_shapes=[
            pltpu.VMEM((rows, cells), x.dtype),
            pltpu.SemaphoreType.DMA((rows // SUB,)),
            pltpu.SemaphoreType.DMA((rows // SUB,)),
        ],
        compiler_params=pltpu.CompilerParams(vmem_limit_bytes=60 * 2**20),
        name="cut",
    )(place[None], x)


def regroup(snapshots):
    n = lax.axis_size("snap")
    me = lax.axis_index("snap")
    cells = snapshots.shape[1] // n
    begin, end = n // 2 + 1, n // 2 + n // 4
    far = [d for d in reversed(range(n // 2, n)) if d not in (begin, end)]
    got = {}
    for d in [end, *range(1, n // 2), *far, begin, 0]:
        if d == begin:
            block = cut(me ^ d, snapshots, cells)
        else:
            block = lax.dynamic_slice_in_dim(snapshots, (me ^ d) * cells, cells, axis=1)
        got[d] = lax.ppermute(block, "snap", [(i, i ^ d) for i in range(n)]) if d else block
    order = [d for d in range(n) if d != end] + [end]
    return me ^ jnp.array(order, dtype=jnp.int32), [got[d] for d in order]


def local(snapshots):
    n = lax.axis_size("snap")
    size, cells = snapshots.shape[0] * n, snapshots.shape[1] // n
    root = math.sqrt(cells * n * lax.axis_size("row"))
    places, parts = regroup(snapshots)
    packed, hi, lo, hi_kept, lo_kept = gram(places, parts[:-1], cells // 8)
    packed, hi_last, lo_last = add_last(places, packed, parts[-1], hi, lo)
    factor, white = factorize(sum_all(packed), size, root)
    return whiten(places, white, hi_kept, lo_kept, hi_last, lo_last, cells // 8, 4), factor


def solution(mesh):
    in_specs = (P("snap", "row"),)
    out_specs = (P(None, ("row", "snap")), P())
    return jax.shard_map(local, mesh=mesh, in_specs=in_specs, out_specs=out_specs, check_vma=False)
```

```python
import functools
import math

import jax
import jax.numpy as jnp
from jax import lax
from jax.experimental import pallas as pl
from jax.experimental.pallas import tpu as pltpu
from jax.sharding import PartitionSpec as P

BLK = 128
SUB = 8
FULL = lax.Precision.HIGHEST
VMEM = pl.BlockSpec(memory_space=pltpu.VMEM)
ANY = pl.BlockSpec(memory_space=pl.ANY)
SMEM = pl.BlockSpec(memory_space=pltpu.SMEM)


def lower_blocks(size):
    return [(i, j) for i in range(size // BLK) for j in range(i + 1)]


def split(x):
    hi = x.astype(jnp.bfloat16)
    return hi, (x - hi.astype(jnp.float32)).astype(jnp.bfloat16)


def nt(a, b):
    return lax.dot_general(a, b, (((1,), (1,)), ((), ())), preferred_element_type=jnp.float32)


def gram_kernel(count, tile, places_ref, *refs):
    parts, (out_ref, hi_ref, lo_ref, hi_out, lo_out, acc, sems) = refs[:count], refs[count:]
    rows, cells = parts[0].shape
    size = hi_ref.shape[0]
    stores = []
    for t in range(cells // tile):
        here = slice(t * tile, (t + 1) * tile)
        for d in range(count + 1):
            at = pl.ds(pl.multiple_of(places_ref[d] * rows, rows), rows)
            if d < count:
                hi_ref[at, here], lo_ref[at, here] = split(parts[d][:, here])
            else:
                hi_ref[at, here] = lo_ref[at, here] = jnp.zeros((rows, tile), jnp.bfloat16)
        for ref, out in ((hi_ref, hi_out), (lo_ref, lo_out)):
            stores.append(pltpu.make_async_copy(ref.at[:, here], out.at[:, here], sems.at[len(stores)]))
            stores[-1].start()
        hi = hi_ref[:, here]
        prod = nt(hi, jnp.concatenate([hi, lo_ref[:, here]], axis=0))
        acc[...] = acc[...] + prod if t else prod
    for n, (i, j) in enumerate(lower_blocks(size)):
        high = acc[i * BLK : (i + 1) * BLK, j * BLK : (j + 1) * BLK]
        mixed = acc[i * BLK : (i + 1) * BLK, size + j * BLK : size + (j + 1) * BLK]
        other = acc[j * BLK : (j + 1) * BLK, size + i * BLK : size + (i + 1) * BLK]
        out_ref[n * BLK : (n + 1) * BLK, :] = high + mixed + other.T
    for store in stores:
        store.wait()


def gram(places, parts, tile):
    rows, cells = parts[0].shape
    n = len(parts)
    size = rows * (n + 1)
    kept = jax.ShapeDtypeStruct((size, cells), jnp.bfloat16)
    return pl.pallas_call(
        functools.partial(gram_kernel, n, tile),
        out_shape=(jax.ShapeDtypeStruct((len(lower_blocks(size)) * BLK, BLK), jnp.float32), *[kept] * 4),
        in_specs=[SMEM, *[VMEM] * n],
        out_specs=(VMEM, VMEM, VMEM, ANY, ANY),
        scratch_shapes=[pltpu.VMEM((size, 2 * size), jnp.float32), pltpu.SemaphoreType.DMA((2 * (cells // tile),))],
        compiler_params=pltpu.CompilerParams(vmem_limit_bytes=32 * 2**20),
        cost_estimate=pl.CostEstimate(flops=4 * size * size * cells, bytes_accessed=8 * size * cells, transcendentals=0),
        name="gram",
    )(places, *parts)


def last_kernel(places_ref, before_ref, part_ref, hi_ref, lo_ref, out_ref, hi_last, lo_last, wide):
    rows = part_ref.shape[0]
    size = hi_ref.shape[0]
    place = places_ref[places_ref.shape[0] - 1]
    at = pl.ds(pl.multiple_of(place * rows, rows), rows)
    hi, lo = hi_last[...], lo_last[...] = split(part_ref[...])
    both = jnp.concatenate([hi, lo], axis=0)
    cross = nt(hi_ref[...], both)
    cross = cross[:, :rows] + cross[:, rows:] + nt(lo_ref[...], hi)
    square = nt(hi, both)
    square = square[:, :rows] * 0.5 + square[:, rows:]
    wide[...] = jnp.zeros_like(wide)
    lane = lax.broadcasted_iota(jnp.int32, (rows, size), 1)
    inside = (lane >= place * rows) & (lane < (place + 1) * rows)
    square = jnp.concatenate([square] * (size // rows), axis=1)
    wide[at, :] = cross.T + jnp.where(inside, square, 0.0)
    for n, (i, j) in enumerate(lower_blocks(size)):
        down = wide[i * BLK : (i + 1) * BLK, j * BLK : (j + 1) * BLK]
        across = wide[j * BLK : (j + 1) * BLK, i * BLK : (i + 1) * BLK]
        out_ref[n * BLK : (n + 1) * BLK, :] = before_ref[n * BLK : (n + 1) * BLK, :] + (down + across.T)


def add_last(places, before, part, hi, lo):
    rows, cells = part.shape
    size = hi.shape[0]
    kept = jax.ShapeDtypeStruct((rows, cells), jnp.bfloat16)
    return pl.pallas_call(
        last_kernel,
        out_shape=(jax.ShapeDtypeStruct(before.shape, jnp.float32), kept, kept),
        in_specs=[SMEM, VMEM, VMEM, VMEM, VMEM],
        out_specs=(VMEM, VMEM, VMEM),
        scratch_shapes=[pltpu.VMEM((size, size), jnp.float32)],
        compiler_params=pltpu.CompilerParams(vmem_limit_bytes=16 * 2**20),
        cost_estimate=pl.CostEstimate(flops=6 * rows * size * cells, bytes_accessed=4 * size * cells, transcendentals=0),
        name="gram_last",
    )(places, before, part, hi, lo)


def bits(axis):
    n = lax.axis_size(axis)
    return [1 << b for b in range(n.bit_length() - 1)]


def step(x, orders, at):
    rows, snaps = lax.axis_size("row"), lax.axis_size("snap")
    pairs = []
    for r in range(rows):
        for s in range(snaps):
            axis, bit = orders[r % 2][at]
            to = (r ^ bit, s) if axis == "row" else (r, s ^ bit)
            pairs.append((s * rows + r, to[1] * rows + to[0]))
    return lax.ppermute(x, ("snap", "row"), pairs)


def side(orders, at):
    core = lax.axis_index("row") % 2
    flags = [(lax.axis_index(axis) & bit) > 0 for axis, bit in (o[at] for o in orders)]
    return jnp.where(core == 0, flags[0], flags[1])


def sum_all(x):
    links = [("row", b) for b in bits("row")[1:]] + [("snap", b) for b in bits("snap")]
    orders = [[("row", 1), *links], [("row", 1), *links[len(links) // 2 :], *links[: len(links) // 2]]]
    for at in (0, 1):
        upper = side(orders, at)
        half = x.shape[0] // 2
        first, second = x[:half], x[half:]
        x = jnp.where(upper, second, first) + step(jnp.where(upper, first, second), orders, at)
    for at in range(2, len(links) + 1):
        x = x + step(x, orders, at)
    for at in (1, 0):
        upper = side(orders, at)
        got = step(x, orders, at)
        x = jnp.where(upper, jnp.concatenate([got, x]), jnp.concatenate([x, got]))
    return x


def spread_columns(x, at):
    return [jnp.broadcast_to(x[:, at + j : at + j + 1], (SUB, BLK)) for j in range(SUB)]


def spread_row(x, j):
    return jnp.broadcast_to(x[j : j + 1, :], (SUB, BLK))


def tree_sum(terms):
    while len(terms) > 1:
        terms = [sum(terms[t : t + 2][1:], terms[t]) for t in range(0, len(terms), 2)]
    return terms[0]


def factor_block(rows):
    groups = len(rows)
    part = groups // 2
    lane = lax.broadcasted_iota(jnp.int32, (SUB, BLK), 1)
    sub = lax.broadcasted_iota(jnp.int32, (SUB, BLK), 0)
    rows = list(rows)
    inverse, upper = [], []

    def gather(wide):
        out = wide[0]
        for j in range(1, SUB):
            out = jnp.where(sub == j, wide[j], out)
        return out

    for k in range(groups):
        base = SUB * k
        end = (k // part + 1) * part
        near = k + 1 < end
        if k % part == 0:
            if k:
                top = jnp.concatenate(inverse[k - part : k], axis=0)
                right = jnp.concatenate(upper[k - part : k], axis=0)
                full = jnp.where(lax.broadcasted_iota(jnp.int32, top.shape, 1) < base, top, right)
                rest = lax.dot_general(
                    right[:, base:], full, (((0,), (0,)), ((), ())), precision=FULL, preferred_element_type=jnp.float32
                )
                for i in range(k, groups):
                    old = jnp.where((lane >= base - SUB * part) & (lane < base), 0.0, rows[i])
                    rows[i] = old - rest[SUB * (i - k) : SUB * (i - k + 1), :]
            spread = spread_columns(rows[k], base)
        if near:
            below = spread_columns(rows[k + 1], base)
            beyond = spread_columns(rows[k + 1], base + SUB)
        cell = {(i, j): spread_row(spread[j], i) for i in range(SUB) for j in range(i + 1)}
        in_block = (lane >= base) & (lane < base + SUB)
        up = [spread_row(rows[k], j) for j in range(SUB)]
        aug = [jnp.where(in_block, jnp.where(lane == base + j, 1.0, 0.0), up[j]) for j in range(SUB)]
        inv, ratio = [], {}
        for j in range(SUB):
            inv.append(pl.reciprocal(cell[j, j], approx=True))
            for i in range(j + 1, SUB):
                ratio[i, j] = cell[i, j] * inv[j]
            for i in range(j + 1, SUB):
                for c in range(j + 1, i + 1):
                    cell[i, c] = cell[i, c] - ratio[i, j] * cell[c, j]

        def eliminate(cols):
            cols = list(cols)
            for j in range(SUB):
                for c in range(j + 1, SUB):
                    cols[c] = cols[c] - cols[j] * ratio[c, j]
            return cols

        def update(i, m):
            rows[i] = jnp.where(in_block, 0.0, rows[i]) - tree_sum([m[j] * aug[j] for j in range(SUB)])

        if near:
            below = eliminate(below)
            m = [below[j] * inv[j] for j in range(SUB)]
            spread = [
                beyond[c] - tree_sum([m[j] * spread_row(below[j], c) for j in range(SUB)]) for c in range(SUB)
            ]
        aug, up = eliminate(aug), eliminate(up)
        if near:
            update(k + 1, m)
        for i in range(k + 2, end):
            cols = eliminate(spread_columns(rows[i], base))
            update(i, [cols[j] * inv[j] for j in range(SUB)])
        scale = lax.rsqrt(gather([cell[j, j] for j in range(SUB)]))
        inverse.append(jnp.where(lane <= base + sub, gather(aug) * scale, 0.0))
        upper.append(jnp.where(lane >= base + sub, gather(up) * scale, 0.0))
    return inverse, upper


def factor_kernel(root, gram_ref, lower_ref, white_ref, work, xs, us):
    size = lower_ref.shape[0]
    blocks = size // BLK
    for n, (i, j) in enumerate(lower_blocks(size)):
        block = gram_ref[n * BLK : (n + 1) * BLK, :]
        work[i * BLK : (i + 1) * BLK, j * BLK : (j + 1) * BLK] = block
        if i != j:
            work[j * BLK : (j + 1) * BLK, i * BLK : (i + 1) * BLK] = block.T
    eye = jnp.where(
        lax.broadcasted_iota(jnp.int32, (BLK, BLK), 0) == lax.broadcasted_iota(jnp.int32, (BLK, BLK), 1), 1.0, 0.0
    )
    zero = jnp.zeros((BLK, BLK), jnp.float32)
    for b in range(blocks):
        here = slice(b * BLK, (b + 1) * BLK)
        inverse, upper = factor_block([work[b * BLK + SUB * i : b * BLK + SUB * (i + 1), here] for i in range(BLK // SUB)])
        for k in range(BLK // SUB):
            xs[SUB * k : SUB * (k + 1), :] = inverse[k]
            us[SUB * k : SUB * (k + 1), :] = upper[k]
        work[here, here] = eye
        y = jnp.dot(xs[...], work[here, :], precision=FULL, preferred_element_type=jnp.float32)
        for i in range(b + 1, blocks):
            down = slice(i * BLK, (i + 1) * BLK)
            left = y[:, down].T
            work[down, here] = zero
            work[down, :] = work[down, :] - jnp.dot(left, y, precision=FULL, preferred_element_type=jnp.float32)
            lower_ref[down, here] = left * (1.0 / root)
            lower_ref[here, down] = zero
            white_ref[here, down] = zero
        lower_ref[here, here] = us[...].T * (1.0 / root)
        white_ref[here, : (b + 1) * BLK] = y[:, : (b + 1) * BLK] * root


def factorize(packed, size, root):
    out = jax.ShapeDtypeStruct((size, size), jnp.float32)
    return pl.pallas_call(
        functools.partial(factor_kernel, root),
        out_shape=(out, out),
        in_specs=[VMEM],
        out_specs=(VMEM, VMEM),
        scratch_shapes=[
            pltpu.VMEM((size, size), jnp.float32),
            pltpu.VMEM((BLK, BLK), jnp.float32),
            pltpu.VMEM((BLK, BLK), jnp.float32),
        ],
        compiler_params=pltpu.CompilerParams(vmem_limit_bytes=12 * 2**20),
        cost_estimate=pl.CostEstimate(flops=100 * size**3, bytes_accessed=8 * size * size, transcendentals=size),
        name="factor",
    )(packed)


def modes_kernel(places_ref, w_ref, hi_ref, lo_ref, hi_last, lo_last, out_ref, w_hi, w_lo, s_hi, s_lo, tiles, sems):
    size, cells = hi_ref.shape
    rows = hi_last.shape[0]
    slots, _, tile = tiles.shape
    half = size // 2
    at = pl.ds(pl.multiple_of(places_ref[places_ref.shape[0] - 1] * rows, rows), rows)
    w_hi[...], w_lo[...] = split(w_ref[...])
    copies = []
    for t in range(cells // tile):
        slot, here = t % slots, slice(t * tile, (t + 1) * tile)
        s_hi[t % 2], s_lo[t % 2] = hi_ref[:, here], lo_ref[:, here]
        s_hi[t % 2, at, :], s_lo[t % 2, at, :] = hi_last[:, here], lo_last[:, here]
        if t >= slots:
            copies[t - slots].wait()
        for out, depth in ((slice(0, half), half), (slice(half, size), size)):
            a, b = w_hi[out, :depth], w_lo[out, :depth]
            hi, lo = s_hi[t % 2, :depth, :], s_lo[t % 2, :depth, :]
            tiles[slot, out, :] = (
                jnp.dot(a, hi, preferred_element_type=jnp.float32)
                + jnp.dot(a, lo, preferred_element_type=jnp.float32)
                + jnp.dot(b, hi, preferred_element_type=jnp.float32)
            )
        copies.append(pltpu.make_async_copy(tiles.at[slot], out_ref.at[:, here], sems.at[slot]))
        copies[t].start()
    for copy in copies[-slots:]:
        copy.wait()


def whiten(places, w, hi, lo, hi_last, lo_last, tile, slots):
    size, cells = hi.shape
    return pl.pallas_call(
        modes_kernel,
        out_shape=jax.ShapeDtypeStruct((size, cells), jnp.float32),
        in_specs=[SMEM, *[VMEM] * 5],
        out_specs=ANY,
        scratch_shapes=[
            pltpu.VMEM((size, size), jnp.bfloat16),
            pltpu.VMEM((size, size), jnp.bfloat16),
            pltpu.VMEM((2, size, tile), jnp.bfloat16),
            pltpu.VMEM((2, size, tile), jnp.bfloat16),
            pltpu.VMEM((slots, size, tile), jnp.float32),
            pltpu.SemaphoreType.DMA((slots,)),
        ],
        compiler_params=pltpu.CompilerParams(vmem_limit_bytes=16 * 2**20),
        name="modes",
    )(places, w, hi, lo, hi_last, lo_last)


def cut_kernel(place_ref, x_ref, out_ref, held, come, go):
    rows, cells = held.shape
    at = pl.ds(pl.multiple_of(place_ref[0] * cells, cells), cells)
    pieces = [slice(SUB * n, SUB * (n + 1)) for n in range(rows // SUB)]
    loads = [pltpu.make_async_copy(x_ref.at[p, at], held.at[p, :], come.at[n]) for n, p in enumerate(pieces)]
    stores = [pltpu.make_async_copy(held.at[p, :], out_ref.at[p, :], go.at[n]) for n, p in enumerate(pieces)]
    for load in loads:
        load.start()
    for load, store in zip(loads, stores, strict=True):
        load.wait()
        store.start()
    for store in stores:
        store.wait()


def cut(place, x, cells):
    rows = x.shape[0]
    return pl.pallas_call(
        cut_kernel,
        out_shape=jax.ShapeDtypeStruct((rows, cells), x.dtype),
        in_specs=[SMEM, ANY],
        out_specs=ANY,
        scratch_shapes=[
            pltpu.VMEM((rows, cells), x.dtype),
            pltpu.SemaphoreType.DMA((rows // SUB,)),
            pltpu.SemaphoreType.DMA((rows // SUB,)),
        ],
        compiler_params=pltpu.CompilerParams(vmem_limit_bytes=60 * 2**20),
        name="cut",
    )(place[None], x)


def regroup(snapshots):
    n = lax.axis_size("snap")
    me = lax.axis_index("snap")
    cells = snapshots.shape[1] // n
    begin, end = n // 2 + 1, n // 2 + n // 4
    far = [d for d in reversed(range(n // 2, n)) if d not in (begin, end)]
    got = {}
    for d in [end, *range(1, n // 2), *far, begin, 0]:
        if d == begin:
            block = cut(me ^ d, snapshots, cells)
        else:
            block = lax.dynamic_slice_in_dim(snapshots, (me ^ d) * cells, cells, axis=1)
        got[d] = lax.ppermute(block, "snap", [(i, i ^ d) for i in range(n)]) if d else block
    order = [d for d in range(n) if d != end] + [end]
    return me ^ jnp.array(order, dtype=jnp.int32), [got[d] for d in order]


def local(snapshots):
    n = lax.axis_size("snap")
    size, cells = snapshots.shape[0] * n, snapshots.shape[1] // n
    root = math.sqrt(cells * n * lax.axis_size("row"))
    places, parts = regroup(snapshots)
    packed, hi, lo, hi_kept, lo_kept = gram(places, parts[:-1], cells // 8)
    packed, hi_last, lo_last = add_last(places, packed, parts[-1], hi, lo)
    factor, white = factorize(sum_all(packed), size, root)
    return whiten(places, white, hi_kept, lo_kept, hi_last, lo_last, cells // 8, 4), factor


def solution(mesh):
    in_specs = (P("snap", "row"),)
    out_specs = (P(None, ("row", "snap")), P())
    return jax.shard_map(local, mesh=mesh, in_specs=in_specs, out_specs=out_specs, check_vma=False)
```

```python
import functools
import math

import jax
import jax.numpy as jnp
from jax import lax
from jax.experimental import pallas as pl
from jax.experimental.pallas import tpu as pltpu
from jax.sharding import PartitionSpec as P

BLK = 128
SUB = 8
FULL = lax.Precision.HIGHEST
VMEM = pl.BlockSpec(memory_space=pltpu.VMEM)
ANY = pl.BlockSpec(memory_space=pl.ANY)
SMEM = pl.BlockSpec(memory_space=pltpu.SMEM)


def lower_blocks(size):
    return [(i, j) for i in range(size // BLK) for j in range(i + 1)]


def split(x):
    hi = x.astype(jnp.bfloat16)
    return hi, (x - hi.astype(jnp.float32)).astype(jnp.bfloat16)


def nt(a, b):
    return lax.dot_general(a, b, (((1,), (1,)), ((), ())), preferred_element_type=jnp.float32)


def gram_kernel(count, tile, places_ref, *refs):
    parts, (out_ref, hi_ref, lo_ref, hi_out, lo_out, acc, sems) = refs[:count], refs[count:]
    rows, cells = parts[0].shape
    size = hi_ref.shape[0]
    stores = []
    for t in range(cells // tile):
        here = slice(t * tile, (t + 1) * tile)
        for d in range(count + 1):
            at = pl.ds(pl.multiple_of(places_ref[d] * rows, rows), rows)
            if d < count:
                hi_ref[at, here], lo_ref[at, here] = split(parts[d][:, here])
            else:
                hi_ref[at, here] = lo_ref[at, here] = jnp.zeros((rows, tile), jnp.bfloat16)
        for ref, out in ((hi_ref, hi_out), (lo_ref, lo_out)):
            stores.append(pltpu.make_async_copy(ref.at[:, here], out.at[:, here], sems.at[len(stores)]))
            stores[-1].start()
        hi = hi_ref[:, here]
        prod = nt(hi, jnp.concatenate([hi, lo_ref[:, here]], axis=0))
        acc[...] = acc[...] + prod if t else prod
    for n, (i, j) in enumerate(lower_blocks(size)):
        high = acc[i * BLK : (i + 1) * BLK, j * BLK : (j + 1) * BLK]
        mixed = acc[i * BLK : (i + 1) * BLK, size + j * BLK : size + (j + 1) * BLK]
        other = acc[j * BLK : (j + 1) * BLK, size + i * BLK : size + (i + 1) * BLK]
        out_ref[n * BLK : (n + 1) * BLK, :] = high + mixed + other.T
    for store in stores:
        store.wait()


def gram(places, parts, tile):
    rows, cells = parts[0].shape
    n = len(parts)
    size = rows * (n + 1)
    kept = jax.ShapeDtypeStruct((size, cells), jnp.bfloat16)
    return pl.pallas_call(
        functools.partial(gram_kernel, n, tile),
        out_shape=(jax.ShapeDtypeStruct((len(lower_blocks(size)) * BLK, BLK), jnp.float32), *[kept] * 4),
        in_specs=[SMEM, *[VMEM] * n],
        out_specs=(VMEM, VMEM, VMEM, ANY, ANY),
        scratch_shapes=[pltpu.VMEM((size, 2 * size), jnp.float32), pltpu.SemaphoreType.DMA((2 * (cells // tile),))],
        compiler_params=pltpu.CompilerParams(vmem_limit_bytes=32 * 2**20),
        cost_estimate=pl.CostEstimate(flops=4 * size * size * cells, bytes_accessed=8 * size * cells, transcendentals=0),
        name="gram",
    )(places, *parts)


def last_kernel(places_ref, before_ref, part_ref, hi_ref, lo_ref, out_ref, hi_last, lo_last, wide):
    rows = part_ref.shape[0]
    size = hi_ref.shape[0]
    place = places_ref[places_ref.shape[0] - 1]
    at = pl.ds(pl.multiple_of(place * rows, rows), rows)
    hi, lo = hi_last[...], lo_last[...] = split(part_ref[...])
    both = jnp.concatenate([hi, lo], axis=0)
    cross = nt(hi_ref[...], both)
    cross = cross[:, :rows] + cross[:, rows:] + nt(lo_ref[...], hi)
    square = nt(hi, both)
    square = square[:, :rows] * 0.5 + square[:, rows:]
    wide[...] = jnp.zeros_like(wide)
    lane = lax.broadcasted_iota(jnp.int32, (rows, size), 1)
    inside = (lane >= place * rows) & (lane < (place + 1) * rows)
    square = jnp.concatenate([square] * (size // rows), axis=1)
    wide[at, :] = cross.T + jnp.where(inside, square, 0.0)
    for n, (i, j) in enumerate(lower_blocks(size)):
        down = wide[i * BLK : (i + 1) * BLK, j * BLK : (j + 1) * BLK]
        across = wide[j * BLK : (j + 1) * BLK, i * BLK : (i + 1) * BLK]
        out_ref[n * BLK : (n + 1) * BLK, :] = before_ref[n * BLK : (n + 1) * BLK, :] + (down + across.T)


def add_last(places, before, part, hi, lo):
    rows, cells = part.shape
    size = hi.shape[0]
    kept = jax.ShapeDtypeStruct((rows, cells), jnp.bfloat16)
    return pl.pallas_call(
        last_kernel,
        out_shape=(jax.ShapeDtypeStruct(before.shape, jnp.float32), kept, kept),
        in_specs=[SMEM, VMEM, VMEM, VMEM, VMEM],
        out_specs=(VMEM, VMEM, VMEM),
        scratch_shapes=[pltpu.VMEM((size, size), jnp.float32)],
        compiler_params=pltpu.CompilerParams(vmem_limit_bytes=16 * 2**20),
        cost_estimate=pl.CostEstimate(flops=6 * rows * size * cells, bytes_accessed=4 * size * cells, transcendentals=0),
        name="gram_last",
    )(places, before, part, hi, lo)


def bits(axis):
    n = lax.axis_size(axis)
    return [1 << b for b in range(n.bit_length() - 1)]


def step(x, orders, at):
    rows, snaps = lax.axis_size("row"), lax.axis_size("snap")
    pairs = []
    for r in range(rows):
        for s in range(snaps):
            axis, bit = orders[r % 2][at]
            to = (r ^ bit, s) if axis == "row" else (r, s ^ bit)
            pairs.append((s * rows + r, to[1] * rows + to[0]))
    return lax.ppermute(x, ("snap", "row"), pairs)


def side(orders, at):
    core = lax.axis_index("row") % 2
    flags = [(lax.axis_index(axis) & bit) > 0 for axis, bit in (o[at] for o in orders)]
    return jnp.where(core == 0, flags[0], flags[1])


def sum_all(x):
    links = [("row", b) for b in bits("row")[1:]] + [("snap", b) for b in bits("snap")]
    orders = [[("row", 1), *links], [("row", 1), *links[1:], links[0]]]
    for at in (0, 1):
        upper = side(orders, at)
        half = x.shape[0] // 2
        first, second = x[:half], x[half:]
        x = jnp.where(upper, second, first) + step(jnp.where(upper, first, second), orders, at)
    for at in range(2, len(links) + 1):
        x = x + step(x, orders, at)
    for at in (1, 0):
        upper = side(orders, at)
        got = step(x, orders, at)
        x = jnp.where(upper, jnp.concatenate([got, x]), jnp.concatenate([x, got]))
    return x


def spread_columns(x, at):
    return [jnp.broadcast_to(x[:, at + j : at + j + 1], (SUB, BLK)) for j in range(SUB)]


def spread_row(x, j):
    return jnp.broadcast_to(x[j : j + 1, :], (SUB, BLK))


def tree_sum(terms):
    while len(terms) > 1:
        terms = [sum(terms[t : t + 2][1:], terms[t]) for t in range(0, len(terms), 2)]
    return terms[0]


def factor_block(rows):
    groups = len(rows)
    part = groups // 2
    lane = lax.broadcasted_iota(jnp.int32, (SUB, BLK), 1)
    sub = lax.broadcasted_iota(jnp.int32, (SUB, BLK), 0)
    rows = list(rows)
    inverse, upper = [], []

    def gather(wide):
        out = wide[0]
        for j in range(1, SUB):
            out = jnp.where(sub == j, wide[j], out)
        return out

    for k in range(groups):
        base = SUB * k
        end = (k // part + 1) * part
        near = k + 1 < end
        if k % part == 0:
            if k:
                top = jnp.concatenate(inverse[k - part : k], axis=0)
                right = jnp.concatenate(upper[k - part : k], axis=0)
                full = jnp.where(lax.broadcasted_iota(jnp.int32, top.shape, 1) < base, top, right)
                rest = lax.dot_general(
                    right[:, base:], full, (((0,), (0,)), ((), ())), precision=FULL, preferred_element_type=jnp.float32
                )
                for i in range(k, groups):
                    old = jnp.where((lane >= base - SUB * part) & (lane < base), 0.0, rows[i])
                    rows[i] = old - rest[SUB * (i - k) : SUB * (i - k + 1), :]
            spread = spread_columns(rows[k], base)
        if near:
            below = spread_columns(rows[k + 1], base)
            beyond = spread_columns(rows[k + 1], base + SUB)
        cell = {(i, j): spread_row(spread[j], i) for i in range(SUB) for j in range(i + 1)}
        in_block = (lane >= base) & (lane < base + SUB)
        up = [spread_row(rows[k], j) for j in range(SUB)]
        aug = [jnp.where(in_block, jnp.where(lane == base + j, 1.0, 0.0), up[j]) for j in range(SUB)]
        inv, ratio = [], {}
        for j in range(SUB):
            inv.append(pl.reciprocal(cell[j, j], approx=True))
            for i in range(j + 1, SUB):
                ratio[i, j] = cell[i, j] * inv[j]
            for i in range(j + 1, SUB):
                for c in range(j + 1, i + 1):
                    cell[i, c] = cell[i, c] - ratio[i, j] * cell[c, j]

        def eliminate(cols):
            cols = list(cols)
            for j in range(SUB):
                for c in range(j + 1, SUB):
                    cols[c] = cols[c] - cols[j] * ratio[c, j]
            return cols

        def update(i, m):
            rows[i] = jnp.where(in_block, 0.0, rows[i]) - tree_sum([m[j] * aug[j] for j in range(SUB)])

        if near:
            below = eliminate(below)
            m = [below[j] * inv[j] for j in range(SUB)]
            spread = [
                beyond[c] - tree_sum([m[j] * spread_row(below[j], c) for j in range(SUB)]) for c in range(SUB)
            ]
        aug, up = eliminate(aug), eliminate(up)
        if near:
            update(k + 1, m)
        for i in range(k + 2, end):
            cols = eliminate(spread_columns(rows[i], base))
            update(i, [cols[j] * inv[j] for j in range(SUB)])
        scale = lax.rsqrt(gather([cell[j, j] for j in range(SUB)]))
        inverse.append(jnp.where(lane <= base + sub, gather(aug) * scale, 0.0))
        upper.append(jnp.where(lane >= base + sub, gather(up) * scale, 0.0))
    return inverse, upper


def factor_kernel(root, gram_ref, lower_ref, white_ref, work, xs, us):
    size = lower_ref.shape[0]
    blocks = size // BLK
    for n, (i, j) in enumerate(lower_blocks(size)):
        block = gram_ref[n * BLK : (n + 1) * BLK, :]
        work[i * BLK : (i + 1) * BLK, j * BLK : (j + 1) * BLK] = block
        if i != j:
            work[j * BLK : (j + 1) * BLK, i * BLK : (i + 1) * BLK] = block.T
    eye = jnp.where(
        lax.broadcasted_iota(jnp.int32, (BLK, BLK), 0) == lax.broadcasted_iota(jnp.int32, (BLK, BLK), 1), 1.0, 0.0
    )
    zero = jnp.zeros((BLK, BLK), jnp.float32)
    for b in range(blocks):
        here = slice(b * BLK, (b + 1) * BLK)
        inverse, upper = factor_block([work[b * BLK + SUB * i : b * BLK + SUB * (i + 1), here] for i in range(BLK // SUB)])
        for k in range(BLK // SUB):
            xs[SUB * k : SUB * (k + 1), :] = inverse[k]
            us[SUB * k : SUB * (k + 1), :] = upper[k]
        work[here, here] = eye
        y = jnp.dot(xs[...], work[here, :], precision=FULL, preferred_element_type=jnp.float32)
        for i in range(b + 1, blocks):
            down = slice(i * BLK, (i + 1) * BLK)
            left = y[:, down].T
            work[down, here] = zero
            work[down, :] = work[down, :] - jnp.dot(left, y, precision=FULL, preferred_element_type=jnp.float32)
            lower_ref[down, here] = left * (1.0 / root)
            lower_ref[here, down] = zero
            white_ref[here, down] = zero
        lower_ref[here, here] = us[...].T * (1.0 / root)
        white_ref[here, : (b + 1) * BLK] = y[:, : (b + 1) * BLK] * root


def factorize(packed, size, root):
    out = jax.ShapeDtypeStruct((size, size), jnp.float32)
    return pl.pallas_call(
        functools.partial(factor_kernel, root),
        out_shape=(out, out),
        in_specs=[VMEM],
        out_specs=(VMEM, VMEM),
        scratch_shapes=[
            pltpu.VMEM((size, size), jnp.float32),
            pltpu.VMEM((BLK, BLK), jnp.float32),
            pltpu.VMEM((BLK, BLK), jnp.float32),
        ],
        compiler_params=pltpu.CompilerParams(vmem_limit_bytes=12 * 2**20),
        cost_estimate=pl.CostEstimate(flops=100 * size**3, bytes_accessed=8 * size * size, transcendentals=size),
        name="factor",
    )(packed)


def modes_kernel(places_ref, w_ref, hi_ref, lo_ref, hi_last, lo_last, out_ref, w_hi, w_lo, s_hi, s_lo, tiles, sems):
    size, cells = hi_ref.shape
    rows = hi_last.shape[0]
    slots, _, tile = tiles.shape
    half = size // 2
    at = pl.ds(pl.multiple_of(places_ref[places_ref.shape[0] - 1] * rows, rows), rows)
    w_hi[...], w_lo[...] = split(w_ref[...])
    copies = []
    for t in range(cells // tile):
        slot, here = t % slots, slice(t * tile, (t + 1) * tile)
        s_hi[t % 2], s_lo[t % 2] = hi_ref[:, here], lo_ref[:, here]
        s_hi[t % 2, at, :], s_lo[t % 2, at, :] = hi_last[:, here], lo_last[:, here]
        if t >= slots:
            copies[t - slots].wait()
        for out, depth in ((slice(0, half), half), (slice(half, size), size)):
            a, b = w_hi[out, :depth], w_lo[out, :depth]
            hi, lo = s_hi[t % 2, :depth, :], s_lo[t % 2, :depth, :]
            tiles[slot, out, :] = (
                jnp.dot(a, hi, preferred_element_type=jnp.float32)
                + jnp.dot(a, lo, preferred_element_type=jnp.float32)
                + jnp.dot(b, hi, preferred_element_type=jnp.float32)
            )
        copies.append(pltpu.make_async_copy(tiles.at[slot], out_ref.at[:, here], sems.at[slot]))
        copies[t].start()
    for copy in copies[-slots:]:
        copy.wait()


def whiten(places, w, hi, lo, hi_last, lo_last, tile, slots):
    size, cells = hi.shape
    return pl.pallas_call(
        modes_kernel,
        out_shape=jax.ShapeDtypeStruct((size, cells), jnp.float32),
        in_specs=[SMEM, *[VMEM] * 5],
        out_specs=ANY,
        scratch_shapes=[
            pltpu.VMEM((size, size), jnp.bfloat16),
            pltpu.VMEM((size, size), jnp.bfloat16),
            pltpu.VMEM((2, size, tile), jnp.bfloat16),
            pltpu.VMEM((2, size, tile), jnp.bfloat16),
            pltpu.VMEM((slots, size, tile), jnp.float32),
            pltpu.SemaphoreType.DMA((slots,)),
        ],
        compiler_params=pltpu.CompilerParams(vmem_limit_bytes=16 * 2**20),
        name="modes",
    )(places, w, hi, lo, hi_last, lo_last)


def cut_kernel(place_ref, x_ref, out_ref, held, come, go):
    rows, cells = held.shape
    at = pl.ds(pl.multiple_of(place_ref[0] * cells, cells), cells)
    pieces = [slice(SUB * n, SUB * (n + 1)) for n in range(rows // SUB)]
    loads = [pltpu.make_async_copy(x_ref.at[p, at], held.at[p, :], come.at[n]) for n, p in enumerate(pieces)]
    stores = [pltpu.make_async_copy(held.at[p, :], out_ref.at[p, :], go.at[n]) for n, p in enumerate(pieces)]
    for load in loads:
        load.start()
    for load, store in zip(loads, stores, strict=True):
        load.wait()
        store.start()
    for store in stores:
        store.wait()


def cut(place, x, cells):
    rows = x.shape[0]
    return pl.pallas_call(
        cut_kernel,
        out_shape=jax.ShapeDtypeStruct((rows, cells), x.dtype),
        in_specs=[SMEM, ANY],
        out_specs=ANY,
        scratch_shapes=[
            pltpu.VMEM((rows, cells), x.dtype),
            pltpu.SemaphoreType.DMA((rows // SUB,)),
            pltpu.SemaphoreType.DMA((rows // SUB,)),
        ],
        compiler_params=pltpu.CompilerParams(vmem_limit_bytes=60 * 2**20),
        name="cut",
    )(place[None], x)


def regroup(snapshots):
    n = lax.axis_size("snap")
    me = lax.axis_index("snap")
    cells = snapshots.shape[1] // n
    begin, end = n // 2, n // 2 + n // 4
    far = [d for d in reversed(range(n // 2, n)) if d not in (begin, end)]
    got = {}
    for d in [end, *range(1, n // 2), *far, begin, 0]:
        if d == begin:
            block = cut(me ^ d, snapshots, cells)
        else:
            block = lax.dynamic_slice_in_dim(snapshots, (me ^ d) * cells, cells, axis=1)
        got[d] = lax.ppermute(block, "snap", [(i, i ^ d) for i in range(n)]) if d else block
    order = [d for d in range(n) if d != end] + [end]
    return me ^ jnp.array(order, dtype=jnp.int32), [got[d] for d in order]


def local(snapshots):
    n = lax.axis_size("snap")
    size, cells = snapshots.shape[0] * n, snapshots.shape[1] // n
    root = math.sqrt(cells * n * lax.axis_size("row"))
    places, parts = regroup(snapshots)
    packed, hi, lo, hi_kept, lo_kept = gram(places, parts[:-1], cells // 8)
    packed, hi_last, lo_last = add_last(places, packed, parts[-1], hi, lo)
    factor, white = factorize(sum_all(packed), size, root)
    return whiten(places, white, hi_kept, lo_kept, hi_last, lo_last, cells // 8, 4), factor


def solution(mesh):
    in_specs = (P("snap", "row"),)
    out_specs = (P(None, ("row", "snap")), P())
    return jax.shard_map(local, mesh=mesh, in_specs=in_specs, out_specs=out_specs, check_vma=False)
```

```python
import functools
import math

import jax
import jax.numpy as jnp
from jax import lax
from jax.experimental import pallas as pl
from jax.experimental.pallas import tpu as pltpu
from jax.sharding import PartitionSpec as P

BLK = 128
SUB = 8
FULL = lax.Precision.HIGHEST
VMEM = pl.BlockSpec(memory_space=pltpu.VMEM)
ANY = pl.BlockSpec(memory_space=pl.ANY)
SMEM = pl.BlockSpec(memory_space=pltpu.SMEM)


def lower_blocks(size):
    return [(i, j) for i in range(size // BLK) for j in range(i + 1)]


def split(x):
    hi = x.astype(jnp.bfloat16)
    return hi, (x - hi.astype(jnp.float32)).astype(jnp.bfloat16)


def nt(a, b):
    return lax.dot_general(a, b, (((1,), (1,)), ((), ())), preferred_element_type=jnp.float32)


def gram_kernel(count, tile, places_ref, *refs):
    parts, (out_ref, hi_ref, lo_ref, hi_out, lo_out, acc, sems) = refs[:count], refs[count:]
    rows, cells = parts[0].shape
    size = hi_ref.shape[0]
    stores = []
    for t in range(cells // tile):
        here = slice(t * tile, (t + 1) * tile)
        for d in range(count + 1):
            at = pl.ds(pl.multiple_of(places_ref[d] * rows, rows), rows)
            if d < count:
                hi_ref[at, here], lo_ref[at, here] = split(parts[d][:, here])
            else:
                hi_ref[at, here] = lo_ref[at, here] = jnp.zeros((rows, tile), jnp.bfloat16)
        for ref, out in ((hi_ref, hi_out), (lo_ref, lo_out)):
            stores.append(pltpu.make_async_copy(ref.at[:, here], out.at[:, here], sems.at[len(stores)]))
            stores[-1].start()
        hi = hi_ref[:, here]
        prod = nt(hi, jnp.concatenate([hi, lo_ref[:, here]], axis=0))
        acc[...] = acc[...] + prod if t else prod
    for n, (i, j) in enumerate(lower_blocks(size)):
        high = acc[i * BLK : (i + 1) * BLK, j * BLK : (j + 1) * BLK]
        mixed = acc[i * BLK : (i + 1) * BLK, size + j * BLK : size + (j + 1) * BLK]
        other = acc[j * BLK : (j + 1) * BLK, size + i * BLK : size + (i + 1) * BLK]
        out_ref[n * BLK : (n + 1) * BLK, :] = high + mixed + other.T
    for store in stores:
        store.wait()


def gram(places, parts, tile):
    rows, cells = parts[0].shape
    n = len(parts)
    size = rows * (n + 1)
    kept = jax.ShapeDtypeStruct((size, cells), jnp.bfloat16)
    return pl.pallas_call(
        functools.partial(gram_kernel, n, tile),
        out_shape=(jax.ShapeDtypeStruct((len(lower_blocks(size)) * BLK, BLK), jnp.float32), *[kept] * 4),
        in_specs=[SMEM, *[VMEM] * n],
        out_specs=(VMEM, VMEM, VMEM, ANY, ANY),
        scratch_shapes=[pltpu.VMEM((size, 2 * size), jnp.float32), pltpu.SemaphoreType.DMA((2 * (cells // tile),))],
        compiler_params=pltpu.CompilerParams(vmem_limit_bytes=32 * 2**20),
        cost_estimate=pl.CostEstimate(flops=4 * size * size * cells, bytes_accessed=8 * size * cells, transcendentals=0),
        name="gram",
    )(places, *parts)


def last_kernel(places_ref, before_ref, part_ref, hi_ref, lo_ref, out_ref, hi_last, lo_last, wide):
    rows = part_ref.shape[0]
    size = hi_ref.shape[0]
    place = places_ref[places_ref.shape[0] - 1]
    at = pl.ds(pl.multiple_of(place * rows, rows), rows)
    hi, lo = hi_last[...], lo_last[...] = split(part_ref[...])
    both = jnp.concatenate([hi, lo], axis=0)
    cross = nt(hi_ref[...], both)
    cross = cross[:, :rows] + cross[:, rows:] + nt(lo_ref[...], hi)
    square = nt(hi, both)
    square = square[:, :rows] * 0.5 + square[:, rows:]
    wide[...] = jnp.zeros_like(wide)
    lane = lax.broadcasted_iota(jnp.int32, (rows, size), 1)
    inside = (lane >= place * rows) & (lane < (place + 1) * rows)
    square = jnp.concatenate([square] * (size // rows), axis=1)
    wide[at, :] = cross.T + jnp.where(inside, square, 0.0)
    for n, (i, j) in enumerate(lower_blocks(size)):
        down = wide[i * BLK : (i + 1) * BLK, j * BLK : (j + 1) * BLK]
        across = wide[j * BLK : (j + 1) * BLK, i * BLK : (i + 1) * BLK]
        out_ref[n * BLK : (n + 1) * BLK, :] = before_ref[n * BLK : (n + 1) * BLK, :] + (down + across.T)


def add_last(places, before, part, hi, lo):
    rows, cells = part.shape
    size = hi.shape[0]
    kept = jax.ShapeDtypeStruct((rows, cells), jnp.bfloat16)
    return pl.pallas_call(
        last_kernel,
        out_shape=(jax.ShapeDtypeStruct(before.shape, jnp.float32), kept, kept),
        in_specs=[SMEM, VMEM, VMEM, VMEM, VMEM],
        out_specs=(VMEM, VMEM, VMEM),
        scratch_shapes=[pltpu.VMEM((size, size), jnp.float32)],
        compiler_params=pltpu.CompilerParams(vmem_limit_bytes=16 * 2**20),
        cost_estimate=pl.CostEstimate(flops=6 * rows * size * cells, bytes_accessed=4 * size * cells, transcendentals=0),
        name="gram_last",
    )(places, before, part, hi, lo)


def bits(axis):
    n = lax.axis_size(axis)
    return [1 << b for b in range(n.bit_length() - 1)]


def step(x, orders, at):
    rows, snaps = lax.axis_size("row"), lax.axis_size("snap")
    pairs = []
    for r in range(rows):
        for s in range(snaps):
            axis, bit = orders[r % 2][at]
            to = (r ^ bit, s) if axis == "row" else (r, s ^ bit)
            pairs.append((s * rows + r, to[1] * rows + to[0]))
    return lax.ppermute(x, ("snap", "row"), pairs)


def side(orders, at):
    core = lax.axis_index("row") % 2
    flags = [(lax.axis_index(axis) & bit) > 0 for axis, bit in (o[at] for o in orders)]
    return jnp.where(core == 0, flags[0], flags[1])


def sum_all(x):
    links = [("row", b) for b in bits("row")[1:]] + [("snap", b) for b in bits("snap")]
    orders = [[("row", 1), *links], [("row", 1), *links[1:], links[0]]]
    for at in (0, 1):
        upper = side(orders, at)
        half = x.shape[0] // 2
        first, second = x[:half], x[half:]
        x = jnp.where(upper, second, first) + step(jnp.where(upper, first, second), orders, at)
    for at in range(2, len(links) + 1):
        x = x + step(x, orders, at)
    for at in (1, 0):
        upper = side(orders, at)
        got = step(x, orders, at)
        x = jnp.where(upper, jnp.concatenate([got, x]), jnp.concatenate([x, got]))
    return x


def spread_columns(x, at):
    return [jnp.broadcast_to(x[:, at + j : at + j + 1], (SUB, BLK)) for j in range(SUB)]


def spread_row(x, j):
    return jnp.broadcast_to(x[j : j + 1, :], (SUB, BLK))


def tree_sum(terms):
    while len(terms) > 1:
        terms = [sum(terms[t : t + 2][1:], terms[t]) for t in range(0, len(terms), 2)]
    return terms[0]


def factor_block(rows):
    groups = len(rows)
    part = groups // 2
    lane = lax.broadcasted_iota(jnp.int32, (SUB, BLK), 1)
    sub = lax.broadcasted_iota(jnp.int32, (SUB, BLK), 0)
    rows = list(rows)
    inverse, upper = [], []

    def gather(wide):
        out = wide[0]
        for j in range(1, SUB):
            out = jnp.where(sub == j, wide[j], out)
        return out

    for k in range(groups):
        base = SUB * k
        end = (k // part + 1) * part
        near = k + 1 < end
        if k % part == 0:
            if k:
                top = jnp.concatenate(inverse[k - part : k], axis=0)
                right = jnp.concatenate(upper[k - part : k], axis=0)
                full = jnp.where(lax.broadcasted_iota(jnp.int32, top.shape, 1) < base, top, right)
                rest = lax.dot_general(
                    right[:, base:], full, (((0,), (0,)), ((), ())), precision=FULL, preferred_element_type=jnp.float32
                )
                for i in range(k, groups):
                    old = jnp.where((lane >= base - SUB * part) & (lane < base), 0.0, rows[i])
                    rows[i] = old - rest[SUB * (i - k) : SUB * (i - k + 1), :]
            spread = spread_columns(rows[k], base)
        if near:
            below = spread_columns(rows[k + 1], base)
            beyond = spread_columns(rows[k + 1], base + SUB)
        cell = {(i, j): spread_row(spread[j], i) for i in range(SUB) for j in range(i + 1)}
        in_block = (lane >= base) & (lane < base + SUB)
        up = [spread_row(rows[k], j) for j in range(SUB)]
        aug = [jnp.where(in_block, jnp.where(lane == base + j, 1.0, 0.0), up[j]) for j in range(SUB)]
        inv, ratio = [], {}
        for j in range(SUB):
            inv.append(pl.reciprocal(cell[j, j], approx=True))
            for i in range(j + 1, SUB):
                ratio[i, j] = cell[i, j] * inv[j]
            for i in range(j + 1, SUB):
                for c in range(j + 1, i + 1):
                    cell[i, c] = cell[i, c] - ratio[i, j] * cell[c, j]

        def eliminate(cols):
            cols = list(cols)
            for j in range(SUB):
                for c in range(j + 1, SUB):
                    cols[c] = cols[c] - cols[j] * ratio[c, j]
            return cols

        def update(i, m):
            rows[i] = jnp.where(in_block, 0.0, rows[i]) - tree_sum([m[j] * aug[j] for j in range(SUB)])

        if near:
            below = eliminate(below)
            m = [below[j] * inv[j] for j in range(SUB)]
            spread = [
                beyond[c] - tree_sum([m[j] * spread_row(below[j], c) for j in range(SUB)]) for c in range(SUB)
            ]
        aug, up = eliminate(aug), eliminate(up)
        if near:
            update(k + 1, m)
        for i in range(k + 2, end):
            cols = eliminate(spread_columns(rows[i], base))
            update(i, [cols[j] * inv[j] for j in range(SUB)])
        scale = lax.rsqrt(gather([cell[j, j] for j in range(SUB)]))
        inverse.append(jnp.where(lane <= base + sub, gather(aug) * scale, 0.0))
        upper.append(jnp.where(lane >= base + sub, gather(up) * scale, 0.0))
    return inverse, upper


def factor_kernel(root, gram_ref, lower_ref, white_hi, white_lo, work, xs, us):
    size = lower_ref.shape[0]
    blocks = size // BLK
    for n, (i, j) in enumerate(lower_blocks(size)):
        block = gram_ref[n * BLK : (n + 1) * BLK, :]
        work[i * BLK : (i + 1) * BLK, j * BLK : (j + 1) * BLK] = block
        if i != j:
            work[j * BLK : (j + 1) * BLK, i * BLK : (i + 1) * BLK] = block.T
    eye = jnp.where(
        lax.broadcasted_iota(jnp.int32, (BLK, BLK), 0) == lax.broadcasted_iota(jnp.int32, (BLK, BLK), 1), 1.0, 0.0
    )
    zero = jnp.zeros((BLK, BLK), jnp.float32)
    for b in range(blocks):
        here = slice(b * BLK, (b + 1) * BLK)
        inverse, upper = factor_block([work[b * BLK + SUB * i : b * BLK + SUB * (i + 1), here] for i in range(BLK // SUB)])
        for k in range(BLK // SUB):
            xs[SUB * k : SUB * (k + 1), :] = inverse[k]
            us[SUB * k : SUB * (k + 1), :] = upper[k]
        work[here, here] = eye
        y = jnp.dot(xs[...], work[here, :], precision=FULL, preferred_element_type=jnp.float32)
        for i in range(b + 1, blocks):
            down = slice(i * BLK, (i + 1) * BLK)
            left = y[:, down].T
            work[down, here] = zero
            work[down, :] = work[down, :] - jnp.dot(left, y, precision=FULL, preferred_element_type=jnp.float32)
            lower_ref[down, here] = left * (1.0 / root)
            lower_ref[here, down] = zero
            white_hi[here, down] = white_lo[here, down] = zero.astype(jnp.bfloat16)
        lower_ref[here, here] = us[...].T * (1.0 / root)
        done = slice(0, (b + 1) * BLK)
        white_hi[here, done], white_lo[here, done] = split(y[:, done] * root)


def factorize(packed, size, root):
    out = jax.ShapeDtypeStruct((size, size), jnp.float32)
    part = jax.ShapeDtypeStruct((size, size), jnp.bfloat16)
    return pl.pallas_call(
        functools.partial(factor_kernel, root),
        out_shape=(out, part, part),
        in_specs=[VMEM],
        out_specs=(VMEM, VMEM, VMEM),
        scratch_shapes=[
            pltpu.VMEM((size, size), jnp.float32),
            pltpu.VMEM((BLK, BLK), jnp.float32),
            pltpu.VMEM((BLK, BLK), jnp.float32),
        ],
        compiler_params=pltpu.CompilerParams(vmem_limit_bytes=12 * 2**20),
        cost_estimate=pl.CostEstimate(flops=100 * size**3, bytes_accessed=8 * size * size, transcendentals=size),
        name="factor",
    )(packed)


def modes_kernel(places_ref, w_hi, w_lo, hi_ref, lo_ref, hi_last, lo_last, out_ref, s_hi, s_lo, tiles, sems):
    size, cells = hi_ref.shape
    rows = hi_last.shape[0]
    slots, _, tile = tiles.shape
    half = size // 2
    at = pl.ds(pl.multiple_of(places_ref[places_ref.shape[0] - 1] * rows, rows), rows)
    copies = []
    for t in range(cells // tile):
        slot, here = t % slots, slice(t * tile, (t + 1) * tile)
        s_hi[t % 2], s_lo[t % 2] = hi_ref[:, here], lo_ref[:, here]
        s_hi[t % 2, at, :], s_lo[t % 2, at, :] = hi_last[:, here], lo_last[:, here]
        if t >= slots:
            copies[t - slots].wait()
        for out, depth in ((slice(0, half), half), (slice(half, size), size)):
            a, b = w_hi[out, :depth], w_lo[out, :depth]
            hi, lo = s_hi[t % 2, :depth, :], s_lo[t % 2, :depth, :]
            tiles[slot, out, :] = (
                jnp.dot(a, hi, preferred_element_type=jnp.float32)
                + jnp.dot(a, lo, preferred_element_type=jnp.float32)
                + jnp.dot(b, hi, preferred_element_type=jnp.float32)
            )
        copies.append(pltpu.make_async_copy(tiles.at[slot], out_ref.at[:, here], sems.at[slot]))
        copies[t].start()
    for copy in copies[-slots:]:
        copy.wait()


def whiten(places, w_hi, w_lo, hi, lo, hi_last, lo_last, tile, slots):
    size, cells = hi.shape
    return pl.pallas_call(
        modes_kernel,
        out_shape=jax.ShapeDtypeStruct((size, cells), jnp.float32),
        in_specs=[SMEM, *[VMEM] * 6],
        out_specs=ANY,
        scratch_shapes=[
            pltpu.VMEM((2, size, tile), jnp.bfloat16),
            pltpu.VMEM((2, size, tile), jnp.bfloat16),
            pltpu.VMEM((slots, size, tile), jnp.float32),
            pltpu.SemaphoreType.DMA((slots,)),
        ],
        compiler_params=pltpu.CompilerParams(vmem_limit_bytes=16 * 2**20),
        name="modes",
    )(places, w_hi, w_lo, hi, lo, hi_last, lo_last)


def cut_kernel(place_ref, x_ref, out_ref, held, come, go):
    rows, cells = held.shape
    at = pl.ds(pl.multiple_of(place_ref[0] * cells, cells), cells)
    pieces = [slice(SUB * n, SUB * (n + 1)) for n in range(rows // SUB)]
    loads = [pltpu.make_async_copy(x_ref.at[p, at], held.at[p, :], come.at[n]) for n, p in enumerate(pieces)]
    stores = [pltpu.make_async_copy(held.at[p, :], out_ref.at[p, :], go.at[n]) for n, p in enumerate(pieces)]
    for load in loads:
        load.start()
    for load, store in zip(loads, stores, strict=True):
        load.wait()
        store.start()
    for store in stores:
        store.wait()


def cut(place, x, cells):
    rows = x.shape[0]
    return pl.pallas_call(
        cut_kernel,
        out_shape=jax.ShapeDtypeStruct((rows, cells), x.dtype),
        in_specs=[SMEM, ANY],
        out_specs=ANY,
        scratch_shapes=[
            pltpu.VMEM((rows, cells), x.dtype),
            pltpu.SemaphoreType.DMA((rows // SUB,)),
            pltpu.SemaphoreType.DMA((rows // SUB,)),
        ],
        compiler_params=pltpu.CompilerParams(vmem_limit_bytes=60 * 2**20),
        name="cut",
    )(place[None], x)


def regroup(snapshots):
    n = lax.axis_size("snap")
    me = lax.axis_index("snap")
    cells = snapshots.shape[1] // n
    begin, end = n // 2, n // 2 + n // 4
    far = [d for d in reversed(range(n // 2, n)) if d not in (begin, end)]
    got = {}
    for d in [end, *range(1, n // 2), *far, begin, 0]:
        if d == begin:
            block = cut(me ^ d, snapshots, cells)
        else:
            block = lax.dynamic_slice_in_dim(snapshots, (me ^ d) * cells, cells, axis=1)
        got[d] = lax.ppermute(block, "snap", [(i, i ^ d) for i in range(n)]) if d else block
    order = [d for d in range(n) if d != end] + [end]
    return me ^ jnp.array(order, dtype=jnp.int32), [got[d] for d in order]


def local(snapshots):
    n = lax.axis_size("snap")
    size, cells = snapshots.shape[0] * n, snapshots.shape[1] // n
    root = math.sqrt(cells * n * lax.axis_size("row"))
    places, parts = regroup(snapshots)
    packed, hi, lo, hi_kept, lo_kept = gram(places, parts[:-1], cells // 8)
    packed, hi_last, lo_last = add_last(places, packed, parts[-1], hi, lo)
    factor, w_hi, w_lo = factorize(sum_all(packed), size, root)
    return whiten(places, w_hi, w_lo, hi_kept, lo_kept, hi_last, lo_last, cells // 8, 4), factor


def solution(mesh):
    in_specs = (P("snap", "row"),)
    out_specs = (P(None, ("row", "snap")), P())
    return jax.shard_map(local, mesh=mesh, in_specs=in_specs, out_specs=out_specs, check_vma=False)
```
